256 devices in a mesh: ctx: 32 (over y_lo, z, core), tp: 8 (over x, y_hi).
Axes of the slice: x: 4, y: 4 (y_hi: 2, y_lo: 2; y = y_hi * 2 + y_lo), z: 8, core: 2. Of those that a mesh axis runs over, the one named last changes fastest.
Arguments:
- queries: bfloat16 [8192, 4096], P('ctx', 'tp'), may hold values from -8 to 8
- key_cache: bfloat16 [131072, 1024], P('ctx', 'tp'), may hold values from -6 to 6
- values: bfloat16 [131072, 1024], P('ctx', 'tp'), may hold values from -6 to 6
- out_weight: bfloat16 [4096, 8192], P('tp'), may hold values from -0.09375 to 0.09375
- selected: int32 [512, 3], P('ctx'), may hold values from -1 to 30, as said below
- shard_order: int32 [32], replicated, may hold values from 0 to 31, each once
Outputs:
- trainer_view: bfloat16 [8192, 8192], P('ctx', 'tp')
The draws below stay inside these ranges and needn't reach their ends.
Inputs may be any that keep to these rules, and one draw needn't show every extreme that they name: `selected`: the blocks a tile names are distinct and lie before the tile's own block; -1 stands for no block. Among the tiles of one block no earlier block is named more than 2 times, and in every draw some block names one exactly 2 times.
All inputs are finite; a program needn't handle non-finite values.
Results may differ from the reference program's by a relative error of at most 0.01555.
Values may be sent and summed in bfloat16 or wider, within the bound.
A program may use at most 128 MiB of HBM per device.

```python
import math
import jax
import jax.numpy as jnp
from jax import lax

D = 8192
H = 32
KVH = 8
DH = 128
BLOCK = 4096
TOPK = 3
TILE = 16
CAP = 2
QROWS = 256
TILES_DEV = 16
NTILES = 512
ROWS = 8192
SEQ = 131072
N_CTX = 32
N_TP = 8


def draw_queries(key, part):
    key = jax.random.fold_in(key, 5)
    base_rows = jnp.clip(jax.random.normal(key, (ROWS, H, DH), jnp.float32), -6.0, 6.0)
    return base_rows.reshape(ROWS, H * DH).astype(jnp.bfloat16)


def draw_key_cache(key, part):
    key = jax.random.fold_in(key, 7)
    base_rows = jnp.clip(jax.random.normal(key, (SEQ, KVH, DH), jnp.float32), -6.0, 6.0)
    return base_rows.reshape(SEQ, KVH * DH).astype(jnp.bfloat16)


def draw_selected(key, part):
    key = jax.random.fold_in(key, 11)
    raw_scores = jax.random.randint(key, (N_CTX, N_CTX), 0, 1024)
    column = jnp.arange(N_CTX)[None, :]
    row_ids = jnp.arange(N_CTX)[:, None]
    ranking = raw_scores * (column + 4) * N_CTX + column
    ranking = jnp.where(column == row_ids - 1, -1, ranking)
    ranking = jnp.where(column < row_ids, ranking, 2 ** 30 + column)
    ordering = jnp.argsort(ranking, axis=1, stable=True).astype(jnp.int32)
    tile_ids = jnp.arange(TILES_DEV)[:, None]
    rank_ids = jnp.arange(TOPK)[None, :]
    counter = (tile_ids * TOPK + rank_ids)[None]
    earlier = jnp.arange(N_CTX)[:, None, None]
    wrapped = counter % jnp.maximum(earlier, 1)
    picked = jnp.take_along_axis(ordering, wrapped.reshape(N_CTX, TILES_DEV * TOPK), axis=1).reshape(N_CTX, TILES_DEV, TOPK)
    usable = (counter < CAP * earlier) & (rank_ids[None] < earlier)
    return jnp.where(usable, picked, -1).reshape(NTILES, TOPK).astype(jnp.int32)


def steps_of(key, extent, cuts, least, top_value):
    loudness, own = 1.0, jax.random.fold_in(key, 6)
    for axis_at, parts in cuts:
        heights = jnp.exp(jax.random.uniform(jax.random.fold_in(own, axis_at), (parts,), jnp.float32, least / len(cuts), top_value / len(cuts)))
        loudness = loudness * jnp.repeat(heights, extent[axis_at] // parts).reshape([-1 if axis == axis_at else 1 for axis in range(len(extent))])
    return loudness


def centred(stream_key, shape, scale, limit, pieces=(), dtype=jnp.bfloat16):
    values = jax.random.normal(stream_key, shape, jnp.float32) * scale
    if len(pieces) > 0:
        values = steps_of(stream_key, shape, pieces, -0.22, 0.18) * values
    return jnp.clip(values, min=-limit, max=limit).astype(dtype)


def setup_inputs(seed: int = 0) -> dict:
    keys = jax.random.split(jax.random.key(seed), 7)
    return {
        "queries": draw_queries(jax.random.fold_in(keys[6], 71), 0),
        "key_cache": draw_key_cache(jax.random.fold_in(keys[6], 71), 0),
        "values": centred(keys[2], (SEQ, KVH * DH), 1.0, 6.0, ((0, 32), (1, 8))),
        "out_weight": centred(keys[3], (H * DH, D), (H * DH) ** -0.5, 0.09375, ((0, 8),)),
        "selected": draw_selected(jax.random.fold_in(keys[6], 71), 0),
        "shard_order": jax.random.permutation(keys[5], N_CTX).astype(jnp.int32),
    }


def partial_attention(query_rows, key_rows, value_rows, visible):
    scores = jnp.einsum('...rd,...kd->...rk', query_rows.astype(jnp.float32), key_rows.astype(jnp.float32), precision=lax.Precision.HIGHEST) * (1.0 / math.sqrt(DH))
    if visible is not None:
        scores = jnp.where(visible, scores, -jnp.inf)
    row_peak = lax.optimization_barrier(jnp.max(scores, axis=-1))
    weights = jnp.exp(scores - row_peak[..., None])
    row_mass = lax.optimization_barrier(jnp.sum(weights, axis=-1))
    rounded = lax.optimization_barrier(weights.astype(jnp.bfloat16)).astype(jnp.float32)
    mixed = jnp.einsum('...rk,...kd->...rd', rounded, value_rows.astype(jnp.float32), precision=lax.Precision.HIGHEST)
    return (mixed / row_mass[..., None], row_peak, row_mass)

def reference(queries, key_cache, values, out_weight, selected, shard_order):
    groups = H // KVH
    tile_count = QROWS // TILE
    query_grid = queries.reshape(N_CTX, QROWS, KVH, groups, DH)
    key_grid = key_cache.reshape(N_CTX, BLOCK, KVH, DH)
    value_grid = values.reshape(N_CTX, BLOCK, KVH, DH)
    choice_grid = selected.reshape(N_CTX, tile_count, TOPK)
    position = BLOCK - QROWS + jnp.arange(QROWS)
    visible = jnp.arange(BLOCK)[None, None, :] <= position[None, :, None]

    def one_block(block_id):
        block_queries = lax.dynamic_index_in_dim(query_grid, block_id, 0, keepdims=False)
        block_keys = lax.dynamic_index_in_dim(key_grid, block_id, 0, keepdims=False)
        block_values = lax.dynamic_index_in_dim(value_grid, block_id, 0, keepdims=False)
        block_choices = lax.dynamic_index_in_dim(choice_grid, block_id, 0, keepdims=False)
        live_flags = (block_choices >= 0)[:, :, None, None]
        safe_choice = jnp.clip(block_choices, 0, N_CTX - 1)

        def one_head(head_id):
            head_queries = lax.dynamic_index_in_dim(block_queries, head_id, 1, keepdims=False).transpose(1, 0, 2)
            own_keys = lax.dynamic_index_in_dim(block_keys, head_id, 1, keepdims=False)
            own_values = lax.dynamic_index_in_dim(block_values, head_id, 1, keepdims=False)
            own_mix, own_peak, own_mass = partial_attention(head_queries, own_keys[None], own_values[None], visible)
            own_mix = own_mix.reshape(groups, tile_count, TILE, DH).transpose(1, 0, 2, 3)
            own_peak = own_peak.reshape(groups, tile_count, TILE).transpose(1, 0, 2)
            own_mass = own_mass.reshape(groups, tile_count, TILE).transpose(1, 0, 2)
            head_keys = lax.dynamic_index_in_dim(key_grid, head_id, 2, keepdims=False)
            head_values = lax.dynamic_index_in_dim(value_grid, head_id, 2, keepdims=False)
            picked_keys = jnp.take(head_keys, safe_choice, axis=0)
            picked_values = jnp.take(head_values, safe_choice, axis=0)
            tile_queries = head_queries.reshape(groups, tile_count, TILE, DH).transpose(1, 0, 2, 3).reshape(tile_count, 1, groups * TILE, DH)
            far_mix, far_peak, far_mass = partial_attention(tile_queries, picked_keys, picked_values, None)
            far_mix = far_mix.reshape(tile_count, TOPK, groups, TILE, DH)
            far_peak = far_peak.reshape(tile_count, TOPK, groups, TILE)
            far_mass = far_mass.reshape(tile_count, TOPK, groups, TILE)
            peak_all = jnp.maximum(own_peak, lax.optimization_barrier(jnp.max(jnp.where(live_flags, far_peak, own_peak[:, None]), axis=1)))
            own_weight = own_mass * jnp.exp(own_peak - peak_all)
            far_weight = jnp.where(live_flags, far_mass * jnp.exp(far_peak - peak_all[:, None]), jnp.float32(0.0))
            numerator = own_weight[..., None] * own_mix + lax.optimization_barrier(jnp.sum(far_weight[..., None] * far_mix, axis=1))
            denominator = own_weight + lax.optimization_barrier(jnp.sum(far_weight, axis=1))
            merged = numerator / denominator[..., None]
            return merged.transpose(0, 2, 1, 3).reshape(QROWS, groups * DH)
        heads_out = lax.map(one_head, jnp.arange(KVH))
        return heads_out.transpose(1, 0, 2).reshape(QROWS, H * DH).astype(jnp.bfloat16)
    attention = lax.map(one_block, jnp.arange(N_CTX)).reshape(ROWS, H * DH)
    head_cols = H * DH // N_TP
    summed = jnp.zeros((ROWS, D), jnp.float32)
    for member in range(N_TP):
        head_term = jnp.dot(attention[:, member * head_cols:(member + 1) * head_cols], out_weight[member * head_cols:(member + 1) * head_cols], preferred_element_type=jnp.float32)
        summed = summed + head_term
    branch = summed.astype(jnp.bfloat16)
    piece_grid = branch.reshape(N_CTX, N_CTX, QROWS // N_CTX, D)
    trainer = jnp.take(piece_grid, shard_order, axis=1).transpose(1, 0, 2, 3).reshape(ROWS, D)
    return trainer
```

```python
import functools
import math

import jax
import jax.numpy as jnp
from jax import lax
from jax.experimental import pallas as pl
from jax.experimental.pallas import tpu as pltpu
from jax.sharding import PartitionSpec as P

DH = 128
TOPK = 3
TILE = 16
CAP = 2
KEYS = 256
UNIT = 4
SCALE = math.log2(math.e) / math.sqrt(DH)
MESH = pl.DeviceIdType.MESH
BF = jnp.bfloat16
F32 = jnp.float32


def iota(shape, dim):
    return lax.broadcasted_iota(jnp.int32, shape, dim)


def dot(a, b):
    return jnp.dot(a, b, preferred_element_type=F32)


def dot_nt(a, b):
    return lax.dot_general(a, b, (((1,), (1,)), ((), ())), preferred_element_type=F32)


def attend(rows, kt, vx, masked):
    count = rows.shape[0]
    scaled = rows.astype(F32) * SCALE
    high = scaled.astype(BF)
    low = (scaled - high.astype(F32)).astype(BF)
    rows = jnp.concatenate([high, low], axis=1)
    steps = vx.shape[0] // KEYS
    peak, total = None, None
    for step in range(steps):
        keys = pl.ds(step * KEYS, KEYS)
        scores = dot(rows, kt[:, keys])
        if masked and step == steps - 1:
            shape = (count, KEYS)
            scores = jnp.where(iota(shape, 1) <= iota(shape, 0) % KEYS, scores, -1e30)
        top = jnp.max(scores, axis=1, keepdims=True)
        if peak is not None:
            top = jnp.maximum(top, peak)
        term = dot(jnp.exp2(scores - top).astype(BF), vx[keys, :])
        total = term if peak is None else total * jnp.exp2(peak - top) + term
        peak = top
    mass = total[:, DH:]
    return total[:, :DH] / mass, peak + jnp.log2(mass)


def kernel(
    n, nt,
    q_ref, sel_ref, order_ref, k_ref, v_ref, w_ref, out_ref,
    kraw, kt, vx, outq, recvq, ret, back, pick, perm, own_mix, own_log,
    wfull, pieces, arrived, ag, acc,
    load_sem, qs_sem, qr_sem, bs_sem, br_sem, ws_sem, wr_sem, fs_sem, fr_sem,
    ts_sem, tr_sem, as_sem, ar_sem,
):
    c = lax.axis_index("ctx")
    t = lax.axis_index("tp")
    core = lax.rem(c, 2)
    sibling = c + 1 - 2 * core
    heads = q_ref.shape[1] // DH
    tiles = sel_ref.shape[0]
    rows = q_ref.shape[0]
    slots = n * CAP
    pair_rows = CAP * TILE
    slot_rows = n * pair_rows
    piece = rows // n
    cols = out_ref.shape[1]
    depth = w_ref.shape[0]
    half = depth // 2

    barrier = pltpu.get_barrier_semaphore()

    def greet_ctx(j, carry):
        pl.semaphore_signal(
            barrier, inc=1, device_id=(lax.rem(c + j, n), t), device_id_type=MESH
        )
        return carry

    lax.fori_loop(1, n, greet_ctx, 0)

    def greet_tp(j, carry):
        pl.semaphore_signal(
            barrier, inc=1, device_id=(c, lax.rem(t + j, nt)), device_id_type=MESH
        )
        return carry

    lax.fori_loop(1, nt, greet_tp, 0)

    load_k = pltpu.make_async_copy(k_ref, kraw, load_sem.at[0])
    load_v = pltpu.make_async_copy(v_ref, vx.at[:, pl.ds(0, DH)], load_sem.at[1])
    load_w = pltpu.make_async_copy(
        w_ref.at[:, pl.ds(pl.multiple_of(t * cols, cols), cols)], wfull.at[t], load_sem.at[2]
    )
    load_k.start()
    load_v.start()
    load_w.start()

    slot_shape = (tiles, slots)
    lane = iota(slot_shape, 1)
    chosen = [sel_ref[:, r : r + 1] for r in range(TOPK)]
    named = [(lane // CAP == chosen[r]) for r in range(TOPK)]
    hit = (named[0] | named[1] | named[2]).astype(F32)
    lower = (iota((tiles, tiles), 1) < iota((tiles, tiles), 0)).astype(BF)
    rank = dot(lower, hit.astype(BF))
    right_rank = (rank == (lane % CAP).astype(F32)).astype(F32)
    owner = (hit * right_rank).astype(BF)
    spread = (iota((tiles, rows), 1) // TILE == iota((tiles, rows), 0)).astype(BF)
    block = 256

    def fill(j, carry):
        base = pl.multiple_of(j * block, block)
        row = base + iota((block, slots), 0)
        of_slot = (row // TILE == iota((block, slots), 1)).astype(BF)
        of_tile = dot_nt(of_slot, owner).astype(BF)
        same = iota((block, rows), 0) % TILE == iota((block, rows), 1) % TILE
        gate = jnp.where(same, dot(of_tile, spread), 0.0).astype(BF)
        outq[pl.ds(base, block), :] = dot(gate, q_ref[...]).astype(BF)
        return carry

    lax.fori_loop(0, slot_rows // block, fill, 0)

    pl.semaphore_wait(barrier, n - 1 + nt - 1)

    def dispatch(k, s, peer=None):
        return pltpu.make_async_remote_copy(
            src_ref=outq.at[pl.ds(pl.multiple_of(k * pair_rows, pair_rows), pair_rows), :],
            dst_ref=recvq.at[s],
            send_sem=qs_sem.at[k],
            recv_sem=qr_sem.at[s],
            device_id=(k if peer is None else peer, t),
            device_id_type=MESH,
        )

    def send_queries(j, carry):
        dispatch(c - 1 - j, c).start()
        return carry

    lax.fori_loop(0, c, send_queries, 0)

    def weight_copy(dest, j):
        return pltpu.make_async_remote_copy(
            src_ref=w_ref.at[
                pl.ds(pl.multiple_of(core * half, half), half),
                pl.ds(pl.multiple_of(dest * cols, cols), cols),
            ],
            dst_ref=wfull.at[t, pl.ds(pl.multiple_of(core * half, half), half), :],
            send_sem=ws_sem.at[j],
            recv_sem=wr_sem.at[j],
            device_id=(c, dest),
            device_id_type=MESH,
        )

    def weight_arrival(source, j):
        view = wfull.at[source, pl.ds(pl.multiple_of(core * half, half), half), :]
        return pltpu.make_async_remote_copy(
            src_ref=view,
            dst_ref=view,
            send_sem=ws_sem.at[j],
            recv_sem=wr_sem.at[j],
            device_id=(c, source),
            device_id_type=MESH,
        )

    def weight_share(source, j, which):
        view = wfull.at[source, pl.ds(pl.multiple_of(which * half, half), half), :]
        return pltpu.make_async_remote_copy(
            src_ref=view,
            dst_ref=view,
            send_sem=fs_sem.at[j],
            recv_sem=fr_sem.at[j],
            device_id=(sibling, t),
            device_id_type=MESH,
        )

    def send_weights(j, carry):
        weight_copy(lax.rem(t + j, nt), j).start()
        return carry

    lax.fori_loop(1, nt, send_weights, 0)

    recvq[c] = jnp.zeros(recvq.shape[1:], BF)

    def clear(k, carry):
        back[pl.ds(pl.multiple_of(k * pair_rows, pair_rows), pair_rows), :] = jnp.zeros(
            (pair_rows, back.shape[1]), BF
        )
        return carry

    lax.fori_loop(c, n, clear, 0)

    load_k.wait()
    kt[0:DH, :] = kraw[...].T
    kt[DH:, :] = kt[0:DH, :]
    load_v.wait()
    vx[:, DH:] = jnp.ones((vx.shape[0], DH), BF)

    for first in range(0, heads, 2):
        pair = jnp.concatenate(
            [q_ref[:, h * DH : (h + 1) * DH] for h in (first, first + 1)], axis=0
        )
        mix, log_mass = attend(pair, kt, vx, True)
        for i, h in enumerate((first, first + 1)):
            own_mix[:, h * DH : (h + 1) * DH] = mix[i * rows : (i + 1) * rows]
            own_log[:, h * DH : (h + 1) * DH] = log_mass[i * rows : (i + 1) * rows]

    def give_back(s, k, peer=None):
        return pltpu.make_async_remote_copy(
            src_ref=ret.at[s],
            dst_ref=back.at[pl.ds(pl.multiple_of(k * pair_rows, pair_rows), pair_rows), :],
            send_sem=bs_sem.at[s],
            recv_sem=br_sem.at[k],
            device_id=(s if peer is None else peer, t),
            device_id_type=MESH,
        )

    def serve(g, carry):
        names = []
        for u in range(UNIT):
            s = c + 1 + g * UNIT + u
            names.append((s, jnp.where(s < n, s, c)))

            @pl.when(s < n)
            def _():
                dispatch(c, s, s).wait_recv()

        parts = []
        for s, at in names:
            held = recvq[at]
            parts += [held[:, h * DH : (h + 1) * DH] for h in range(heads)]
        mix, log_mass = attend(jnp.concatenate(parts, axis=0), kt, vx, False)
        spot = iota((pair_rows, DH), 1)
        for u, (s, at) in enumerate(names):
            base = u * heads * pair_rows
            stat = jnp.zeros((pair_rows, DH), F32)
            for h in range(heads):
                here = slice(base + h * pair_rows, base + (h + 1) * pair_rows)
                ret[at, :, h * DH : (h + 1) * DH] = mix[here].astype(BF)
                stat = jnp.where(spot % heads == h, log_mass[here], stat)
            high = stat.astype(BF).astype(F32)
            middle = (stat - high).astype(BF).astype(F32)
            low = stat - high - middle
            packed = jnp.where(spot < heads, high, jnp.where(spot < 2 * heads, middle, low))
            packed = jnp.where(spot < 3 * heads, packed, 0.0)
            ret[at, :, heads * DH :] = packed.astype(BF)

            @pl.when(s < n)
            def _():
                give_back(s, c).start()

        return carry

    lax.fori_loop(0, (n - 1 - c + UNIT - 1) // UNIT, serve, 0)

    for r in range(TOPK):
        mine = (named[r].astype(F32) * right_rank).astype(BF)
        of_row = dot(
            (iota((rows, tiles), 0) // TILE == iota((rows, tiles), 1)).astype(BF), mine
        ).astype(BF)
        to_slot = (iota((slots, slot_rows), 1) // TILE == iota((slots, slot_rows), 0)).astype(BF)
        same = iota((rows, slot_rows), 0) % TILE == iota((rows, slot_rows), 1) % TILE
        pick[r] = jnp.where(same, dot(of_row, to_slot), 0.0).astype(BF)
    wanted = (iota((n, n), 0) == order_ref[...]).astype(BF)
    row2 = iota((2 * rows, n), 0)
    of_shard = (row2 // (2 * piece) == iota((2 * rows, n), 1)).astype(BF)
    of_piece = dot_nt(of_shard, wanted).astype(BF)
    to_rows = (iota((n, rows), 1) // piece == iota((n, rows), 0)).astype(BF)
    same = iota((2 * rows, rows), 0) % piece == iota((2 * rows, rows), 1) % piece
    perm[...] = jnp.where(same, dot(of_piece, to_rows), 0.0).astype(BF)

    def share(j, carry):
        source = lax.rem(t + nt - j, nt)
        weight_arrival(source, j).wait_recv()
        weight_share(source, j, core).start()
        return carry

    lax.fori_loop(1, nt, share, 0)

    def await_back(j, carry):
        give_back(c, c - 1 - j, c - 1 - j).wait_recv()
        return carry

    lax.fori_loop(0, c, await_back, 0)
    to_heads = (
        (iota((DH, heads * DH), 0) % heads == iota((DH, heads * DH), 1) // DH)
        & (iota((DH, heads * DH), 0) < 3 * heads)
    ).astype(BF)
    row_of = (iota((rows, tiles), 0) // TILE == iota((rows, tiles), 1)).astype(BF)
    logs, mixes = [own_log[...]], [own_mix[...]]
    for r in range(TOPK):
        taken = dot(pick[r], back[...])
        live = dot(row_of, jnp.broadcast_to((chosen[r] >= 0).astype(F32), (tiles, heads * DH)).astype(BF))
        log_mass = dot(taken[:, heads * DH :].astype(BF), to_heads)
        logs.append(jnp.where(live > 0.5, log_mass, -1e30))
        mixes.append(taken[:, : heads * DH])
    top = jnp.maximum(jnp.maximum(logs[0], logs[1]), jnp.maximum(logs[2], logs[3]))
    numerator, denominator = 0.0, 0.0
    for log_mass, mix in zip(logs, mixes):
        weight = jnp.exp2(log_mass - top)
        numerator = numerator + weight * mix
        denominator = denominator + weight
    attention = (numerator / denominator).astype(BF)

    mid = heads * DH // 2
    left = dot(perm[...], attention[:, :mid])
    right = dot(perm[...], attention[:, mid:])
    side = iota((2 * rows, mid), 0) // piece % 2
    pieces[...] = jnp.where(side == 0, left, right).astype(BF)
    size = 2 * piece

    def deliver(d, s):
        return pltpu.make_async_remote_copy(
            src_ref=pieces.at[pl.ds(pl.multiple_of(d * size, size), size), :],
            dst_ref=arrived.at[pl.ds(pl.multiple_of(s * size, size), size), :],
            send_sem=ts_sem.at[d],
            recv_sem=tr_sem.at[s],
            device_id=(d, t),
            device_id_type=MESH,
        )

    def send_piece(j, carry):
        deliver(lax.rem(c + j, n), c).start()
        return carry

    lax.fori_loop(1, n, send_piece, 0)
    here = pl.ds(pl.multiple_of(c * size, size), size)
    arrived[here, :] = pieces[here, :]

    def await_piece(j, carry):
        s = lax.rem(c + n - j, n)
        pltpu.make_async_remote_copy(
            src_ref=arrived.at[pl.ds(pl.multiple_of(s * size, size), size), :],
            dst_ref=arrived.at[pl.ds(pl.multiple_of(s * size, size), size), :],
            send_sem=ts_sem.at[s],
            recv_sem=tr_sem.at[s],
            device_id=(s, t),
            device_id_type=MESH,
        ).wait_recv()
        return carry

    lax.fori_loop(1, n, await_piece, 0)
    split = arrived[...].astype(F32).reshape(n, 2, piece, mid)
    ag[t, :, :mid] = split[:, 0].reshape(rows, mid).astype(BF)
    ag[t, :, mid:] = split[:, 1].reshape(rows, mid).astype(BF)

    ring = nt // 2
    x, y = t // 2, lax.rem(t, 2)
    after, before, across = lax.rem(x + 1, ring), lax.rem(x + ring - 1, ring), 1 - y
    opposite = lax.rem(x + 2, ring)
    middle_row = rows // 2

    def tp_copy(which, part, dest, send, recv):
        if part is None:
            view = ag.at[which]
        else:
            view = ag.at[which, pl.ds(part * middle_row, middle_row), :]
        return pltpu.make_async_remote_copy(
            src_ref=view,
            dst_ref=view,
            send_sem=as_sem.at[send],
            recv_sem=ar_sem.at[which, recv],
            device_id=(c, dest),
            device_id_type=MESH,
        )

    sent = []

    def start(*spec):
        copy = tp_copy(*spec)
        copy.start()
        sent.append(copy)

    def project(which, first=False):
        term = dot(ag[which], wfull[which])
        acc[...] = term if first else acc[...] + term

    start(t, None, after * 2 + y, 0, 0)
    start(t, None, before * 2 + y, 1, 0)
    start(t, None, x * 2 + across, 2, 0)
    load_w.wait()

    def await_share(j, carry):
        weight_share(lax.rem(t + nt - j, nt), j, 1 - core).wait_recv()
        return carry

    lax.fori_loop(1, nt, await_share, 0)
    project(t, True)
    low, high, over = before * 2 + y, after * 2 + y, x * 2 + across
    tp_copy(low, None, low, 0, 0).wait_recv()
    start(low, 0, after * 2 + y, 3, 0)
    tp_copy(high, None, high, 0, 0).wait_recv()
    start(high, 1, before * 2 + y, 4, 1)
    tp_copy(over, None, over, 0, 0).wait_recv()
    start(over, None, after * 2 + y, 5, 0)
    start(over, None, before * 2 + y, 6, 0)
    project(low)
    project(high)
    project(over)
    low2, high2 = before * 2 + across, after * 2 + across
    tp_copy(low2, None, low, 0, 0).wait_recv()
    start(low2, 0, after * 2 + y, 7, 0)
    tp_copy(high2, None, high, 0, 0).wait_recv()
    start(high2, 1, before * 2 + y, 8, 1)
    far, far2 = opposite * 2 + y, opposite * 2 + across
    tp_copy(far, 0, low, 0, 0).wait_recv()
    tp_copy(far, 1, high, 0, 1).wait_recv()
    project(low2)
    project(high2)
    project(far)
    tp_copy(far2, 0, low, 0, 0).wait_recv()
    tp_copy(far2, 1, high, 0, 1).wait_recv()
    out_ref[...] = (acc[...] + dot(ag[far2], wfull[far2])).astype(BF)

    for copy in sent:
        copy.wait_send()

    def drain_ctx(j, carry):
        deliver(lax.rem(c + j, n), c).wait_send()
        return carry

    lax.fori_loop(1, n, drain_ctx, 0)

    def drain_queries(k, carry):
        dispatch(k, c).wait_send()
        return carry

    lax.fori_loop(0, c, drain_queries, 0)

    def drain_back(s, carry):
        give_back(s, c).wait_send()
        return carry

    lax.fori_loop(c + 1, n, drain_back, 0)

    def drain_weights(j, carry):
        weight_copy(lax.rem(t + j, nt), j).wait_send()
        weight_share(lax.rem(t + nt - j, nt), j, core).wait_send()
        return carry

    lax.fori_loop(1, nt, drain_weights, 0)


def local(queries, key_cache, values, out_weight, selected, shard_order):
    n, nt = lax.axis_size("ctx"), lax.axis_size("tp")
    rows, width = queries.shape
    keys = key_cache.shape[0]
    depth, model = out_weight.shape
    cols = model // nt
    pair_rows = CAP * TILE
    dma = pltpu.SemaphoreType.DMA
    vmem = pl.BlockSpec(memory_space=pltpu.VMEM)
    hbm = pl.BlockSpec(memory_space=pl.ANY)
    return pl.pallas_call(
        functools.partial(kernel, n, nt),
        out_shape=jax.ShapeDtypeStruct((rows, cols), BF),
        in_specs=[vmem, vmem, vmem, hbm, hbm, hbm],
        out_specs=vmem,
        scratch_shapes=[
            pltpu.VMEM((keys, DH), BF),
            pltpu.VMEM((2 * DH, keys), BF),
            pltpu.VMEM((keys, 2 * DH), BF),
            pltpu.VMEM((n * pair_rows, width), BF),
            pltpu.VMEM((n, pair_rows, width), BF),
            pltpu.VMEM((n, pair_rows, width + DH), BF),
            pltpu.VMEM((n * pair_rows, width + DH), BF),
            pltpu.VMEM((TOPK, rows, n * pair_rows), BF),
            pltpu.VMEM((2 * rows, rows), BF),
            pltpu.VMEM((rows, width), F32),
            pltpu.VMEM((rows, width), F32),
            pltpu.VMEM((nt, depth, cols), BF),
            pltpu.VMEM((2 * rows, width // 2), BF),
            pltpu.VMEM((2 * rows, width // 2), BF),
            pltpu.VMEM((nt, rows, width), BF),
            pltpu.VMEM((rows, cols), F32),
            dma((3,)), dma((n,)), dma((n,)), dma((n,)), dma((n,)),
            dma((nt,)), dma((nt,)), dma((nt,)), dma((nt,)),
            dma((n,)), dma((n,)), dma((9,)), dma((nt, 2)),
        ],
        compiler_params=pltpu.CompilerParams(
            collective_id=0, has_side_effects=True, vmem_limit_bytes=58 * 2**20
        ),
        name="sublayer",
    )(queries, selected, shard_order.reshape(1, n), key_cache, values, out_weight)


def solution(mesh):
    placed = (P("ctx", "tp"), P("ctx", "tp"), P("ctx", "tp"), P("tp", None), P("ctx", None), P())
    return jax.shard_map(
        local, mesh=mesh, in_specs=placed, out_specs=P("ctx", "tp"), check_vma=False
    )
```

```python
import functools
import math

import jax
import jax.numpy as jnp
from jax import lax
from jax.experimental import pallas as pl
from jax.experimental.pallas import tpu as pltpu
from jax.sharding import PartitionSpec as P

DH = 128
TOPK = 3
TILE = 16
CAP = 2
KEYS = 256
UNIT = 4
SCALE = math.log2(math.e) / math.sqrt(DH)
MESH = pl.DeviceIdType.MESH
BF = jnp.bfloat16
F32 = jnp.float32


def iota(shape, dim):
    return lax.broadcasted_iota(jnp.int32, shape, dim)


def dot(a, b):
    return jnp.dot(a, b, preferred_element_type=F32)


def dot_nt(a, b):
    return lax.dot_general(a, b, (((1,), (1,)), ((), ())), preferred_element_type=F32)


def attend(rows, kt, vx, masked):
    count = rows.shape[0]
    scaled = rows.astype(F32) * SCALE
    high = scaled.astype(BF)
    low = (scaled - high.astype(F32)).astype(BF)
    rows = jnp.concatenate([high, low], axis=1)
    steps = vx.shape[0] // KEYS
    peak, total = None, None
    for step in range(steps):
        keys = pl.ds(step * KEYS, KEYS)
        scores = dot(rows, kt[:, keys])
        if masked and step == steps - 1:
            shape = (count, KEYS)
            scores = jnp.where(iota(shape, 1) <= iota(shape, 0) % KEYS, scores, -1e30)
        top = jnp.max(scores, axis=1, keepdims=True)
        if peak is not None:
            top = jnp.maximum(top, peak)
        term = dot(jnp.exp2(scores - top).astype(BF), vx[keys, :])
        total = term if peak is None else total * jnp.exp2(peak - top) + term
        peak = top
    mass = total[:, DH:]
    return total[:, :DH] / mass, peak + jnp.log2(mass)


def kernel(
    n, nt,
    q_ref, sel_ref, order_ref, k_ref, v_ref, w_ref, out_ref,
    kraw, kt, vx, outq, recvq, ret, back, pick, perm, own_mix, own_log,
    wfull, pieces, arrived, ag, term_out, term_in, acc,
    load_sem, qs_sem, qr_sem, bs_sem, br_sem, ws_sem, wr_sem, fs_sem, fr_sem,
    ts_sem, tr_sem, ys_sem, yr_sem, xs_sem, xr_sem,
):
    c = lax.axis_index("ctx")
    t = lax.axis_index("tp")
    core = lax.rem(c, 2)
    sibling = c + 1 - 2 * core
    heads = q_ref.shape[1] // DH
    tiles = sel_ref.shape[1]
    rows = q_ref.shape[0]
    slots = n * CAP
    pair_rows = CAP * TILE
    slot_rows = n * pair_rows
    piece = rows // n
    cols = out_ref.shape[1]
    depth = w_ref.shape[0]
    half = depth // 2

    barrier = pltpu.get_barrier_semaphore()

    def greet_ctx(j, carry):
        pl.semaphore_signal(
            barrier, inc=1, device_id=(lax.rem(c + j, n), t), device_id_type=MESH
        )
        return carry

    lax.fori_loop(1, n, greet_ctx, 0)

    ring = nt // 2
    x, y = t // 2, lax.rem(t, 2)
    across = x * 2 + 1 - y

    def greet_x(j, carry):
        pl.semaphore_signal(
            barrier, inc=1, device_id=(c, lax.rem(x + j, ring) * 2 + y), device_id_type=MESH
        )
        return carry

    lax.fori_loop(1, ring, greet_x, 0)
    pl.semaphore_signal(barrier, inc=1, device_id=(c, across), device_id_type=MESH)

    load_k = pltpu.make_async_copy(k_ref, kraw, load_sem.at[0])
    load_v = pltpu.make_async_copy(v_ref, vx.at[:, pl.ds(0, DH)], load_sem.at[1])
    load_k.start()
    load_v.start()

    slot_shape = (tiles, slots)
    lane = iota(slot_shape, 1)
    square = (tiles, tiles)
    chosen = [
        jnp.sum(
            jnp.where(iota(square, 0) == iota(square, 1), sel_ref[r : r + 1, :].astype(F32), 0.0),
            axis=1,
            keepdims=True,
        ).astype(jnp.int32)
        for r in range(TOPK)
    ]
    named = [(lane // CAP == chosen[r]) for r in range(TOPK)]
    hit = (named[0] | named[1] | named[2]).astype(F32)
    lower = (iota((tiles, tiles), 1) < iota((tiles, tiles), 0)).astype(BF)
    rank = dot(lower, hit.astype(BF))
    right_rank = (rank == (lane % CAP).astype(F32)).astype(F32)
    owner = (hit * right_rank).astype(BF)
    spread = (iota((tiles, rows), 1) // TILE == iota((tiles, rows), 0)).astype(BF)
    block = 256

    def fill(j, carry):
        base = pl.multiple_of(j * block, block)
        row = base + iota((block, slots), 0)
        of_slot = (row // TILE == iota((block, slots), 1)).astype(BF)
        of_tile = dot_nt(of_slot, owner).astype(BF)
        same = iota((block, rows), 0) % TILE == iota((block, rows), 1) % TILE
        gate = jnp.where(same, dot(of_tile, spread), 0.0).astype(BF)
        outq[pl.ds(base, block), :] = dot(gate, q_ref[...]).astype(BF)
        return carry

    lax.fori_loop(0, slot_rows // block, fill, 0)

    pl.semaphore_wait(barrier, n - 1 + ring - 1 + 1)

    def dispatch(k, s, peer=None):
        return pltpu.make_async_remote_copy(
            src_ref=outq.at[pl.ds(pl.multiple_of(k * pair_rows, pair_rows), pair_rows), :],
            dst_ref=recvq.at[s],
            send_sem=qs_sem.at[k],
            recv_sem=qr_sem.at[s],
            device_id=(k if peer is None else peer, t),
            device_id_type=MESH,
        )

    def send_queries(j, carry):
        dispatch(j, c).start()
        return carry

    lax.fori_loop(0, c, send_queries, 0)

    def columns(dest):
        return pl.ds(pl.multiple_of(dest * 2 * cols, 2 * cols), 2 * cols)

    my_half = pl.ds(pl.multiple_of(core * half, half), half)
    its_half = pl.ds(pl.multiple_of((1 - core) * half, half), half)
    weight_load = pltpu.make_async_copy(w_ref.at[:, columns(x)], wfull.at[x], load_sem.at[2])
    weight_load.start()

    def weight_copy(dest):
        return pltpu.make_async_remote_copy(
            src_ref=w_ref.at[my_half, columns(dest)],
            dst_ref=wfull.at[x, my_half, :],
            send_sem=ws_sem.at[dest],
            recv_sem=wr_sem.at[x],
            device_id=(c, dest * 2 + y),
            device_id_type=MESH,
        )

    def weight_arrival(source):
        view = wfull.at[source, my_half, :]
        return pltpu.make_async_remote_copy(
            src_ref=view,
            dst_ref=view,
            send_sem=ws_sem.at[source],
            recv_sem=wr_sem.at[source],
            device_id=(c, source * 2 + y),
            device_id_type=MESH,
        )

    def weight_share(source, rows_of):
        view = wfull.at[source, rows_of, :]
        return pltpu.make_async_remote_copy(
            src_ref=view,
            dst_ref=view,
            send_sem=fs_sem.at[source],
            recv_sem=fr_sem.at[source],
            device_id=(sibling, t),
            device_id_type=MESH,
        )

    def send_weights(j, carry):
        weight_copy(lax.rem(x + j, ring)).start()
        return carry

    lax.fori_loop(1, ring, send_weights, 0)

    recvq[c] = jnp.zeros(recvq.shape[1:], BF)

    def clear(k, carry):
        back[k] = jnp.zeros(back.shape[1:], BF)
        return carry

    lax.fori_loop(c, n, clear, 0)

    for r in range(TOPK):
        mine = (named[r].astype(F32) * right_rank).astype(BF)
        of_row = dot(
            (iota((rows, tiles), 0) // TILE == iota((rows, tiles), 1)).astype(BF), mine
        ).astype(BF)
        to_slot = (iota((slots, slot_rows), 1) // TILE == iota((slots, slot_rows), 0)).astype(BF)
        same = iota((rows, slot_rows), 0) % TILE == iota((rows, slot_rows), 1) % TILE
        pick[r] = jnp.where(same, dot(of_row, to_slot), 0.0).astype(BF)
    wanted = (iota((n, n), 0) == order_ref[...]).astype(BF)
    row2 = iota((2 * rows, n), 0)
    of_shard = (row2 // (2 * piece) == iota((2 * rows, n), 1)).astype(BF)
    of_piece = dot_nt(of_shard, wanted).astype(BF)
    to_rows = (iota((n, rows), 1) // piece == iota((n, rows), 0)).astype(BF)
    same = iota((2 * rows, rows), 0) % piece == iota((2 * rows, rows), 1) % piece
    perm[...] = jnp.where(same, dot(of_piece, to_rows), 0.0).astype(BF)

    load_k.wait()
    kt[0:DH, :] = kraw[...].T
    kt[DH:, :] = kt[0:DH, :]
    load_v.wait()
    vx[:, DH:] = jnp.ones((vx.shape[0], DH), BF)

    for first in range(0, heads, 2):
        pair = jnp.concatenate(
            [q_ref[:, h * DH : (h + 1) * DH] for h in (first, first + 1)], axis=0
        )
        mix, log_mass = attend(pair, kt, vx, True)
        for i, h in enumerate((first, first + 1)):
            own_mix[:, h * DH : (h + 1) * DH] = mix[i * rows : (i + 1) * rows]
            own_log[:, h * DH : (h + 1) * DH] = log_mass[i * rows : (i + 1) * rows]

    def give_back(s, k, peer=None):
        return pltpu.make_async_remote_copy(
            src_ref=ret.at[s],
            dst_ref=back.at[k],
            send_sem=bs_sem.at[s],
            recv_sem=br_sem.at[k],
            device_id=(s if peer is None else peer, t),
            device_id_type=MESH,
        )

    def serve(g, carry):
        names = []
        for u in range(UNIT):
            s = c + 1 + g * UNIT + u
            names.append((s, jnp.where(s < n, s, c)))

            @pl.when(s < n)
            def _():
                dispatch(c, s, s).wait_recv()

        parts = []
        for s, at in names:
            held = recvq[at]
            parts += [held[:, h * DH : (h + 1) * DH] for h in range(heads)]
        mix, log_mass = attend(jnp.concatenate(parts, axis=0), kt, vx, False)
        spot = iota((TILE, DH), 1)
        for u, (s, at) in enumerate(names):
            base = u * heads * pair_rows
            ret[at, : heads * pair_rows, :] = mix[base : base + heads * pair_rows].astype(BF)
            stat = jnp.zeros((TILE, DH), F32)
            for i in range(CAP):
                for h in range(heads):
                    first = base + h * pair_rows + i * TILE
                    here = (spot // (3 * heads) == i) & (spot % heads == h)
                    stat = jnp.where(here, log_mass[first : first + TILE], stat)
            high = stat.astype(BF).astype(F32)
            middle = (stat - high).astype(BF).astype(F32)
            low = stat - high - middle
            part = spot % (3 * heads) // heads
            packed = jnp.where(part == 0, high, jnp.where(part == 1, middle, low))
            ret[at, heads * pair_rows :, :] = packed.astype(BF)

            @pl.when(s < n)
            def _():
                give_back(s, c).start()

        return carry

    groups = (n - 1 - c + UNIT - 1) // UNIT
    turn = jnp.minimum(groups, (c + 11) // UNIT)
    lax.fori_loop(0, turn, serve, 0)

    def await_back(j, carry):
        give_back(c, c - 1 - j, c - 1 - j).wait_recv()
        return carry

    lax.fori_loop(0, c, await_back, 0)
    to_heads = (
        (iota((DH, heads * DH), 0) % heads == iota((DH, heads * DH), 1) // DH)
        & (iota((DH, heads * DH), 0) < 3 * heads * CAP)
    ).astype(BF)
    row_of = (iota((rows, tiles), 0) // TILE == iota((rows, tiles), 1)).astype(BF)
    stats = back[:, heads * pair_rows :, :]
    stat_lane = iota(stats.shape, 2) // (3 * heads)
    stats = jnp.concatenate(
        [jnp.where(stat_lane == i, stats.astype(F32), 0.0).astype(BF) for i in range(CAP)], axis=1
    ).reshape(slot_rows, DH)
    logs, mixes = [own_log[...]], [own_mix[...]]
    for r in range(TOPK):
        live = dot(row_of, jnp.broadcast_to((chosen[r] >= 0).astype(F32), (tiles, heads * DH)).astype(BF))
        log_mass = dot(dot(pick[r], stats).astype(BF), to_heads)
        logs.append(jnp.where(live > 0.5, log_mass, -1e30))
        mixes.append(
            jnp.concatenate(
                [
                    dot(
                        pick[r],
                        back[:, h * pair_rows : (h + 1) * pair_rows, :].reshape(slot_rows, DH),
                    )
                    for h in range(heads)
                ],
                axis=1,
            )
        )
    top = jnp.maximum(jnp.maximum(logs[0], logs[1]), jnp.maximum(logs[2], logs[3]))
    numerator, denominator = 0.0, 0.0
    for log_mass, mix in zip(logs, mixes):
        weight = jnp.exp2(log_mass - top)
        numerator = numerator + weight * mix
        denominator = denominator + weight
    attention = (numerator / denominator).astype(BF)

    mid = heads * DH // 2
    left = dot(perm[...], attention[:, :mid])
    right = dot(perm[...], attention[:, mid:])
    side = iota((2 * rows, mid), 0) // piece % 2
    pieces[...] = jnp.where(side == 0, left, right).astype(BF)
    size = 2 * piece

    def deliver(d, s):
        return pltpu.make_async_remote_copy(
            src_ref=pieces.at[pl.ds(pl.multiple_of(d * size, size), size), :],
            dst_ref=arrived.at[pl.ds(pl.multiple_of(s * size, size), size), :],
            send_sem=ts_sem.at[d],
            recv_sem=tr_sem.at[s],
            device_id=(d, t),
            device_id_type=MESH,
        )

    def send_piece(j, carry):
        deliver(lax.rem(c + j, n), c).start()
        return carry

    lax.fori_loop(1, n, send_piece, 0)
    here = pl.ds(pl.multiple_of(c * size, size), size)
    arrived[here, :] = pieces[here, :]

    lax.fori_loop(turn, groups, serve, 0)

    def share(j, carry):
        source = lax.rem(x + j, ring)
        weight_arrival(source).wait_recv()
        weight_share(source, my_half).start()
        return carry

    lax.fori_loop(1, ring, share, 0)

    def await_piece(s, carry):
        view = arrived.at[pl.ds(pl.multiple_of(s * size, size), size), :]

        @pl.when(s != c)
        def _():
            pltpu.make_async_remote_copy(
                src_ref=view,
                dst_ref=view,
                send_sem=ts_sem.at[s],
                recv_sem=tr_sem.at[s],
                device_id=(s, t),
                device_id_type=MESH,
            ).wait_recv()

        return carry

    def head_copy(g, which, send, peer):
        begin, count = bounds[g]
        view = ag.at[which, pl.ds(begin * piece, count * piece), :]
        return pltpu.make_async_remote_copy(
            src_ref=view,
            dst_ref=view,
            send_sem=xs_sem.at[g, send],
            recv_sem=xr_sem.at[g, which],
            device_id=(c, peer * 2 + y),
            device_id_type=MESH,
        )

    def term_copy(g):
        begin, count = bounds[g]
        some = pl.ds(begin * piece, count * piece)
        return pltpu.make_async_remote_copy(
            src_ref=term_out.at[some, :],
            dst_ref=term_in.at[some, :],
            send_sem=ys_sem.at[g],
            recv_sem=yr_sem.at[g],
            device_id=(c, across),
            device_id_type=MESH,
        )

    def gather_heads(g):
        begin, count = bounds[g]
        lax.fori_loop(begin, begin + count, await_piece, 0)
        split = arrived[begin * size : (begin + count) * size, :].astype(F32)
        split = split.reshape(count, 2, piece, mid)
        some = slice(begin * piece, (begin + count) * piece)
        ag[x, some, :mid] = split[:, 0].reshape(count * piece, mid).astype(BF)
        ag[x, some, mid:] = split[:, 1].reshape(count * piece, mid).astype(BF)
        for j in range(1, ring):
            dest = lax.rem(x + j, ring)
            head_copy(g, x, dest, dest).start()

    def project(g):
        begin, count = bounds[g]
        some = slice(begin * piece, (begin + count) * piece)
        for j in range(1, ring):
            source = lax.rem(x + j, ring)
            head_copy(g, source, source, source).wait_recv()

        def term(half_y):
            where = pl.ds(pl.multiple_of(half_y * cols, cols), cols)
            total = dot(ag[0, some, :], wfull[0, :, where])
            for source in range(1, ring):
                total = total + dot(ag[source, some, :], wfull[source, :, where])
            return total

        term_out[some, :] = term(1 - y).astype(BF)
        term_copy(g).start()
        acc[some, :] = term(y)

    def finish(g):
        begin, count = bounds[g]
        some = slice(begin * piece, (begin + count) * piece)
        term_copy(g).wait_recv()
        out_ref[some, :] = (acc[some, :] + term_in[some, :].astype(F32)).astype(BF)

    bounds = ((0, n // 2), (n // 2, n // 4), (n * 3 // 4, n // 4))
    gather_heads(0)
    weight_load.wait()

    def await_weights(j, carry):
        weight_share(lax.rem(x + j, ring), its_half).wait_recv()
        return carry

    lax.fori_loop(1, ring, await_weights, 0)
    gather_heads(1)
    project(0)
    gather_heads(2)
    project(1)
    project(2)
    for g in range(len(bounds)):
        finish(g)

    for g in range(len(bounds)):
        term_copy(g).wait_send()
        for j in range(1, ring):
            dest = lax.rem(x + j, ring)
            head_copy(g, x, dest, dest).wait_send()

    def drain_ctx(j, carry):
        deliver(lax.rem(c + j, n), c).wait_send()
        return carry

    lax.fori_loop(1, n, drain_ctx, 0)

    def drain_queries(k, carry):
        dispatch(k, c).wait_send()
        return carry

    lax.fori_loop(0, c, drain_queries, 0)

    def drain_back(s, carry):
        give_back(s, c).wait_send()
        return carry

    lax.fori_loop(c + 1, n, drain_back, 0)

    def drain_weights(j, carry):
        peer = lax.rem(x + j, ring)
        weight_copy(peer).wait_send()
        weight_share(peer, my_half).wait_send()
        return carry

    lax.fori_loop(1, ring, drain_weights, 0)


def local(queries, key_cache, values, out_weight, selected, shard_order):
    n, nt = lax.axis_size("ctx"), lax.axis_size("tp")
    rows, width = queries.shape
    keys = key_cache.shape[0]
    depth, model = out_weight.shape
    cols = model // nt
    pair_rows = CAP * TILE
    heads = width // DH
    dma = pltpu.SemaphoreType.DMA
    vmem = pl.BlockSpec(memory_space=pltpu.VMEM)
    hbm = pl.BlockSpec(memory_space=pl.ANY)
    return pl.pallas_call(
        functools.partial(kernel, n, nt),
        out_shape=jax.ShapeDtypeStruct((rows, cols), BF),
        in_specs=[vmem, vmem, vmem, hbm, hbm, hbm],
        out_specs=vmem,
        scratch_shapes=[
            pltpu.VMEM((keys, DH), BF),
            pltpu.VMEM((2 * DH, keys), BF),
            pltpu.VMEM((keys, 2 * DH), BF),
            pltpu.VMEM((n * pair_rows, width), BF),
            pltpu.VMEM((n, pair_rows, width), BF),
            pltpu.VMEM((n, heads * pair_rows + TILE, DH), BF),
            pltpu.VMEM((n, heads * pair_rows + TILE, DH), BF),
            pltpu.VMEM((TOPK, rows, n * pair_rows), BF),
            pltpu.VMEM((2 * rows, rows), BF),
            pltpu.VMEM((rows, width), F32),
            pltpu.VMEM((rows, width), F32),
            pltpu.VMEM((nt // 2, depth, 2 * cols), BF),
            pltpu.VMEM((2 * rows, width // 2), BF),
            pltpu.VMEM((2 * rows, width // 2), BF),
            pltpu.VMEM((nt // 2, rows, width), BF),
            pltpu.VMEM((rows, cols), BF),
            pltpu.VMEM((rows, cols), BF),
            pltpu.VMEM((rows, cols), F32),
            dma((3,)), dma((n,)), dma((n,)), dma((n,)), dma((n,)),
            dma((nt // 2,)), dma((nt // 2,)), dma((nt // 2,)), dma((nt // 2,)),
            dma((n,)), dma((n,)), dma((3,)), dma((3,)), dma((3, nt // 2)), dma((3, nt // 2)),
        ],
        compiler_params=pltpu.CompilerParams(
            collective_id=0, has_side_effects=True, vmem_limit_bytes=58 * 2**20
        ),
        name="sublayer",
    )(queries, selected.T, shard_order.reshape(1, n), key_cache, values, out_weight)


def solution(mesh):
    placed = (P("ctx", "tp"), P("ctx", "tp"), P("ctx", "tp"), P("tp", None), P("ctx", None), P())
    return jax.shard_map(
        local, mesh=mesh, in_specs=placed, out_specs=P("ctx", "tp"), check_vma=False
    )
```

```python
import functools
import math

import jax
import jax.numpy as jnp
from jax import lax
from jax.experimental import pallas as pl
from jax.experimental.pallas import tpu as pltpu
from jax.sharding import PartitionSpec as P

DH = 128
TOPK = 3
TILE = 16
CAP = 2
KEYS = 256
UNIT = 4
SCALE = math.log2(math.e) / math.sqrt(DH)
MESH = pl.DeviceIdType.MESH
BF = jnp.bfloat16
F32 = jnp.float32


def iota(shape, dim):
    return lax.broadcasted_iota(jnp.int32, shape, dim)


def dot(a, b):
    return jnp.dot(a, b, preferred_element_type=F32)


def dot_nt(a, b):
    return lax.dot_general(a, b, (((1,), (1,)), ((), ())), preferred_element_type=F32)


def attend(rows, kt, vx, masked):
    count = rows.shape[0]
    scaled = rows.astype(F32) * SCALE
    high = scaled.astype(BF)
    low = (scaled - high.astype(F32)).astype(BF)
    rows = jnp.concatenate([high, low], axis=1)
    steps = vx.shape[0] // KEYS
    peak, total = None, None
    for step in range(steps):
        keys = pl.ds(step * KEYS, KEYS)
        scores = dot(rows, kt[:, keys])
        if masked and step == steps - 1:
            shape = (count, KEYS)
            scores = jnp.where(iota(shape, 1) <= iota(shape, 0) % KEYS, scores, -1e30)
        top = jnp.max(scores, axis=1, keepdims=True)
        if peak is not None:
            top = jnp.maximum(top, peak)
        term = dot(jnp.exp2(scores - top).astype(BF), vx[keys, :])
        total = term if peak is None else total * jnp.exp2(peak - top) + term
        peak = top
    mass = total[:, DH:]
    return total[:, :DH] / mass, peak + jnp.log2(mass)


def kernel(
    n, nt,
    q_ref, sel_ref, order_ref, k_ref, v_ref, w_ref, out_ref,
    kraw, kt, vx, outq, recvq, ret, back, pick, perm, own_mix, own_log,
    wfull, pieces, arrived, ag, term_out, term_in, acc,
    load_sem, qs_sem, qr_sem, bs_sem, br_sem, ws_sem, wr_sem, fs_sem, fr_sem,
    ts_sem, tr_sem, ys_sem, yr_sem, xs_sem, xr_sem,
):
    c = lax.axis_index("ctx")
    t = lax.axis_index("tp")
    core = lax.rem(c, 2)
    sibling = c + 1 - 2 * core
    heads = q_ref.shape[1] // DH
    tiles = sel_ref.shape[1]
    rows = q_ref.shape[0]
    slots = n * CAP
    pair_rows = CAP * TILE
    slot_rows = n * pair_rows
    piece = rows // n
    cols = out_ref.shape[1]
    depth = w_ref.shape[0]
    half = depth // 2

    barrier = pltpu.get_barrier_semaphore()

    def greet_ctx(j, carry):
        pl.semaphore_signal(
            barrier, inc=1, device_id=(lax.rem(c + j, n), t), device_id_type=MESH
        )
        return carry

    for j in range(1, n):
        greet_ctx(j, 0)

    ring = nt // 2
    x, y = t // 2, lax.rem(t, 2)
    across = x * 2 + 1 - y

    def greet_x(j, carry):
        pl.semaphore_signal(
            barrier, inc=1, device_id=(c, lax.rem(x + j, ring) * 2 + y), device_id_type=MESH
        )
        return carry

    lax.fori_loop(1, ring, greet_x, 0)
    pl.semaphore_signal(barrier, inc=1, device_id=(c, across), device_id_type=MESH)

    load_k = pltpu.make_async_copy(k_ref, kraw, load_sem.at[0])
    load_v = pltpu.make_async_copy(v_ref, vx.at[:, pl.ds(0, DH)], load_sem.at[1])
    load_k.start()
    load_v.start()

    slot_shape = (tiles, slots)
    lane = iota(slot_shape, 1)
    square = (tiles, tiles)
    chosen = [
        jnp.sum(
            jnp.where(iota(square, 0) == iota(square, 1), sel_ref[r : r + 1, :].astype(F32), 0.0),
            axis=1,
            keepdims=True,
        ).astype(jnp.int32)
        for r in range(TOPK)
    ]
    named = [(lane // CAP == chosen[r]) for r in range(TOPK)]
    hit = (named[0] | named[1] | named[2]).astype(F32)
    lower = (iota((tiles, tiles), 1) < iota((tiles, tiles), 0)).astype(BF)
    rank = dot(lower, hit.astype(BF))
    right_rank = (rank == (lane % CAP).astype(F32)).astype(F32)
    owner = (hit * right_rank).astype(BF)
    spread = (iota((tiles, rows), 1) // TILE == iota((tiles, rows), 0)).astype(BF)
    block = 256

    def fill(j, carry):
        base = pl.multiple_of(j * block, block)
        row = base + iota((block, slots), 0)
        of_slot = (row // TILE == iota((block, slots), 1)).astype(BF)
        of_tile = dot_nt(of_slot, owner).astype(BF)
        same = iota((block, rows), 0) % TILE == iota((block, rows), 1) % TILE
        gate = jnp.where(same, dot(of_tile, spread), 0.0).astype(BF)
        outq[pl.ds(base, block), :] = dot(gate, q_ref[...]).astype(BF)
        return carry

    lax.fori_loop(0, slot_rows // block, fill, 0)

    pl.semaphore_wait(barrier, n - 1 + ring - 1 + 1)

    def dispatch(k, s, peer=None):
        return pltpu.make_async_remote_copy(
            src_ref=outq.at[pl.ds(pl.multiple_of(k * pair_rows, pair_rows), pair_rows), :],
            dst_ref=recvq.at[s],
            send_sem=qs_sem.at[k],
            recv_sem=qr_sem.at[s],
            device_id=(k if peer is None else peer, t),
            device_id_type=MESH,
        )

    def send_queries(j, carry):
        dispatch(c - 1 - j, c).start()
        return carry

    lax.fori_loop(0, c, send_queries, 0)

    def columns(dest):
        return pl.ds(pl.multiple_of(dest * 2 * cols, 2 * cols), 2 * cols)

    my_half = pl.ds(pl.multiple_of(core * half, half), half)
    its_half = pl.ds(pl.multiple_of((1 - core) * half, half), half)
    weight_load = pltpu.make_async_copy(w_ref.at[:, columns(x)], wfull.at[x], load_sem.at[2])
    weight_load.start()

    def weight_copy(dest):
        return pltpu.make_async_remote_copy(
            src_ref=w_ref.at[my_half, columns(dest)],
            dst_ref=wfull.at[x, my_half, :],
            send_sem=ws_sem.at[dest],
            recv_sem=wr_sem.at[x],
            device_id=(c, dest * 2 + y),
            device_id_type=MESH,
        )

    def weight_arrival(source):
        view = wfull.at[source, my_half, :]
        return pltpu.make_async_remote_copy(
            src_ref=view,
            dst_ref=view,
            send_sem=ws_sem.at[source],
            recv_sem=wr_sem.at[source],
            device_id=(c, source * 2 + y),
            device_id_type=MESH,
        )

    def weight_share(source, rows_of):
        view = wfull.at[source, rows_of, :]
        return pltpu.make_async_remote_copy(
            src_ref=view,
            dst_ref=view,
            send_sem=fs_sem.at[source],
            recv_sem=fr_sem.at[source],
            device_id=(sibling, t),
            device_id_type=MESH,
        )

    def send_weights(j, carry):
        weight_copy(lax.rem(x + j, ring)).start()
        return carry

    lax.fori_loop(1, ring, send_weights, 0)

    recvq[c] = jnp.zeros(recvq.shape[1:], BF)

    def clear(k, carry):
        back[k] = jnp.zeros(back.shape[1:], BF)
        return carry

    lax.fori_loop(c, n, clear, 0)

    for r in range(TOPK):
        mine = (named[r].astype(F32) * right_rank).astype(BF)
        of_row = dot(
            (iota((rows, tiles), 0) // TILE == iota((rows, tiles), 1)).astype(BF), mine
        ).astype(BF)
        to_slot = (iota((slots, slot_rows), 1) // TILE == iota((slots, slot_rows), 0)).astype(BF)
        same = iota((rows, slot_rows), 0) % TILE == iota((rows, slot_rows), 1) % TILE
        pick[r * rows : (r + 1) * rows, :] = jnp.where(same, dot(of_row, to_slot), 0.0).astype(BF)
    wanted = (iota((n, n), 0) == order_ref[...]).astype(BF)
    row2 = iota((2 * rows, n), 0)
    of_shard = (row2 // (2 * piece) == iota((2 * rows, n), 1)).astype(BF)
    of_piece = dot_nt(of_shard, wanted).astype(BF)
    to_rows = (iota((n, rows), 1) // piece == iota((n, rows), 0)).astype(BF)
    same = iota((2 * rows, rows), 0) % piece == iota((2 * rows, rows), 1) % piece
    perm[...] = jnp.where(same, dot(of_piece, to_rows), 0.0).astype(BF)

    load_k.wait()
    kt[0:DH, :] = kraw[...].T
    kt[DH:, :] = kt[0:DH, :]
    load_v.wait()
    vx[:, DH:] = jnp.ones((vx.shape[0], DH), BF)

    for first in range(0, heads, 2):
        pair = jnp.concatenate(
            [q_ref[:, h * DH : (h + 1) * DH] for h in (first, first + 1)], axis=0
        )
        mix, log_mass = attend(pair, kt, vx, True)
        for i, h in enumerate((first, first + 1)):
            own_mix[:, h * DH : (h + 1) * DH] = mix[i * rows : (i + 1) * rows]
            own_log[:, h * DH : (h + 1) * DH] = log_mass[i * rows : (i + 1) * rows]

    def give_back(s, k, peer=None):
        return pltpu.make_async_remote_copy(
            src_ref=ret.at[s],
            dst_ref=back.at[k],
            send_sem=bs_sem.at[s],
            recv_sem=br_sem.at[k],
            device_id=(s if peer is None else peer, t),
            device_id_type=MESH,
        )

    def serve(g, carry):
        names = []
        for u in range(UNIT):
            s = c + 1 + g * UNIT + u
            names.append((s, jnp.where(s < n, s, c)))

            @pl.when(s < n)
            def _():
                dispatch(c, s, s).wait_recv()

        parts = []
        for s, at in names:
            held = recvq[at]
            parts += [held[:, h * DH : (h + 1) * DH] for h in range(heads)]
        mix, log_mass = attend(jnp.concatenate(parts, axis=0), kt, vx, False)
        spot = iota((TILE, DH), 1)
        for u, (s, at) in enumerate(names):
            base = u * heads * pair_rows
            ret[at, : heads * pair_rows, :] = mix[base : base + heads * pair_rows].astype(BF)
            stat = jnp.zeros((TILE, DH), F32)
            for i in range(CAP):
                for h in range(heads):
                    first = base + h * pair_rows + i * TILE
                    here = (spot // (3 * heads) == i) & (spot % heads == h)
                    stat = jnp.where(here, log_mass[first : first + TILE], stat)
            high = stat.astype(BF).astype(F32)
            middle = (stat - high).astype(BF).astype(F32)
            low = stat - high - middle
            part = spot % (3 * heads) // heads
            packed = jnp.where(part == 0, high, jnp.where(part == 1, middle, low))
            ret[at, heads * pair_rows :, :] = packed.astype(BF)

            @pl.when(s < n)
            def _():
                give_back(s, c).start()

        return carry

    groups = (n - 1 - c + UNIT - 1) // UNIT
    turn = jnp.minimum(groups, (c + 11) // UNIT)
    lax.fori_loop(0, turn, serve, 0)

    def await_back(j, carry):
        give_back(c, c - 1 - j, c - 1 - j).wait_recv()
        return carry

    lax.fori_loop(0, c, await_back, 0)
    to_heads = (
        (iota((DH, heads * DH), 0) % heads == iota((DH, heads * DH), 1) // DH)
        & (iota((DH, heads * DH), 0) < 3 * heads * CAP)
    ).astype(BF)
    row_of = (iota((rows, tiles), 0) // TILE == iota((rows, tiles), 1)).astype(BF)
    stats = back[:, heads * pair_rows :, :]
    stat_lane = iota(stats.shape, 2) // (3 * heads)
    stats = jnp.concatenate(
        [jnp.where(stat_lane == i, stats.astype(F32), 0.0).astype(BF) for i in range(CAP)], axis=1
    ).reshape(slot_rows, DH)
    wide = [
        back[:, h * pair_rows : (h + 1) * pair_rows, :].reshape(slot_rows, DH) for h in range(heads)
    ]
    taken = dot(pick[...], jnp.concatenate(wide, axis=1))
    taken_log = dot(dot(pick[...], stats).astype(BF), to_heads)
    logs, mixes = [own_log[...]], [own_mix[...]]
    for r in range(TOPK):
        some = slice(r * rows, (r + 1) * rows)
        live = dot(row_of, jnp.broadcast_to((chosen[r] >= 0).astype(F32), (tiles, heads * DH)).astype(BF))
        logs.append(jnp.where(live > 0.5, taken_log[some], -1e30))
        mixes.append(taken[some])
    top = jnp.maximum(jnp.maximum(logs[0], logs[1]), jnp.maximum(logs[2], logs[3]))
    numerator, denominator = 0.0, 0.0
    for log_mass, mix in zip(logs, mixes):
        weight = jnp.exp2(log_mass - top)
        numerator = numerator + weight * mix
        denominator = denominator + weight
    attention = (numerator / denominator).astype(BF)

    mid = heads * DH // 2
    left = dot(perm[...], attention[:, :mid])
    right = dot(perm[...], attention[:, mid:])
    side = iota((2 * rows, mid), 0) // piece % 2
    pieces[...] = jnp.where(side == 0, left, right).astype(BF)
    size = 2 * piece

    def deliver(d, s):
        return pltpu.make_async_remote_copy(
            src_ref=pieces.at[pl.ds(pl.multiple_of(d * size, size), size), :],
            dst_ref=arrived.at[pl.ds(pl.multiple_of(s * size, size), size), :],
            send_sem=ts_sem.at[d],
            recv_sem=tr_sem.at[s],
            device_id=(d, t),
            device_id_type=MESH,
        )

    def send_piece(j, carry):
        deliver(lax.rem(c + j, n), c).start()
        return carry

    for j in range(1, n):
        send_piece(j, 0)
    here = pl.ds(pl.multiple_of(c * size, size), size)
    arrived[here, :] = pieces[here, :]

    lax.fori_loop(turn, groups, serve, 0)

    def share(j, carry):
        source = lax.rem(x + j, ring)
        weight_arrival(source).wait_recv()
        weight_share(source, my_half).start()
        return carry

    lax.fori_loop(1, ring, share, 0)

    def await_piece(s, carry):
        view = arrived.at[pl.ds(pl.multiple_of(s * size, size), size), :]

        @pl.when(s != c)
        def _():
            pltpu.make_async_remote_copy(
                src_ref=view,
                dst_ref=view,
                send_sem=ts_sem.at[s],
                recv_sem=tr_sem.at[s],
                device_id=(s, t),
                device_id_type=MESH,
            ).wait_recv()

        return carry

    def head_copy(g, which, send, peer):
        begin, count = bounds[g]
        view = ag.at[which, pl.ds(begin * piece, count * piece), :]
        return pltpu.make_async_remote_copy(
            src_ref=view,
            dst_ref=view,
            send_sem=xs_sem.at[g, send],
            recv_sem=xr_sem.at[g, which],
            device_id=(c, peer * 2 + y),
            device_id_type=MESH,
        )

    def term_copy(g):
        begin, count = bounds[g]
        some = pl.ds(begin * piece, count * piece)
        return pltpu.make_async_remote_copy(
            src_ref=term_out.at[some, :],
            dst_ref=term_in.at[some, :],
            send_sem=ys_sem.at[g],
            recv_sem=yr_sem.at[g],
            device_id=(c, across),
            device_id_type=MESH,
        )

    def gather_heads(g):
        begin, count = bounds[g]
        lax.fori_loop(begin, begin + count, await_piece, 0)
        split = arrived[begin * size : (begin + count) * size, :].astype(F32)
        split = split.reshape(count, 2, piece, mid)
        some = slice(begin * piece, (begin + count) * piece)
        ag[x, some, :mid] = split[:, 0].reshape(count * piece, mid).astype(BF)
        ag[x, some, mid:] = split[:, 1].reshape(count * piece, mid).astype(BF)
        for j in range(1, ring):
            dest = lax.rem(x + j, ring)
            head_copy(g, x, dest, dest).start()

    def project(g):
        begin, count = bounds[g]
        some = slice(begin * piece, (begin + count) * piece)
        for j in range(1, ring):
            source = lax.rem(x + j, ring)
            head_copy(g, source, source, source).wait_recv()

        def term(half_y):
            where = pl.ds(pl.multiple_of(half_y * cols, cols), cols)
            total = dot(ag[0, some, :], wfull[0, :, where])
            for source in range(1, ring):
                total = total + dot(ag[source, some, :], wfull[source, :, where])
            return total

        term_out[some, :] = term(1 - y).astype(BF)
        term_copy(g).start()
        acc[some, :] = term(y)

    def finish(g):
        begin, count = bounds[g]
        some = slice(begin * piece, (begin + count) * piece)
        term_copy(g).wait_recv()
        out_ref[some, :] = (acc[some, :] + term_in[some, :].astype(F32)).astype(BF)

    bounds = ((0, n // 2), (n // 2, n // 4), (n * 3 // 4, n // 4))
    def drain_queries(k, carry):
        dispatch(k, c).wait_send()
        return carry

    lax.fori_loop(0, c, drain_queries, 0)

    def drain_back(s, carry):
        give_back(s, c).wait_send()
        return carry

    lax.fori_loop(c + 1, n, drain_back, 0)
    gather_heads(0)
    weight_load.wait()

    def await_weights(j, carry):
        weight_share(lax.rem(x + j, ring), its_half).wait_recv()
        return carry

    lax.fori_loop(1, ring, await_weights, 0)
    gather_heads(1)
    project(0)
    gather_heads(2)
    def drain_ctx(j, carry):
        deliver(lax.rem(c + j, n), c).wait_send()
        return carry

    lax.fori_loop(1, n, drain_ctx, 0)
    project(1)
    project(2)
    for g in range(len(bounds)):
        finish(g)

    for g in range(len(bounds)):
        term_copy(g).wait_send()
        for j in range(1, ring):
            dest = lax.rem(x + j, ring)
            head_copy(g, x, dest, dest).wait_send()

    def drain_weights(j, carry):
        peer = lax.rem(x + j, ring)
        weight_copy(peer).wait_send()
        weight_share(peer, my_half).wait_send()
        return carry

    lax.fori_loop(1, ring, drain_weights, 0)


def local(queries, key_cache, values, out_weight, selected, shard_order):
    n, nt = lax.axis_size("ctx"), lax.axis_size("tp")
    rows, width = queries.shape
    keys = key_cache.shape[0]
    depth, model = out_weight.shape
    cols = model // nt
    pair_rows = CAP * TILE
    heads = width // DH
    dma = pltpu.SemaphoreType.DMA
    vmem = pl.BlockSpec(memory_space=pltpu.VMEM)
    hbm = pl.BlockSpec(memory_space=pl.ANY)
    return pl.pallas_call(
        functools.partial(kernel, n, nt),
        out_shape=jax.ShapeDtypeStruct((rows, cols), BF),
        in_specs=[vmem, vmem, vmem, hbm, hbm, hbm],
        out_specs=vmem,
        scratch_shapes=[
            pltpu.VMEM((keys, DH), BF),
            pltpu.VMEM((2 * DH, keys), BF),
            pltpu.VMEM((keys, 2 * DH), BF),
            pltpu.VMEM((n * pair_rows, width), BF),
            pltpu.VMEM((n, pair_rows, width), BF),
            pltpu.VMEM((n, heads * pair_rows + TILE, DH), BF),
            pltpu.VMEM((n, heads * pair_rows + TILE, DH), BF),
            pltpu.VMEM((TOPK * rows, n * pair_rows), BF),
            pltpu.VMEM((2 * rows, rows), BF),
            pltpu.VMEM((rows, width), F32),
            pltpu.VMEM((rows, width), F32),
            pltpu.VMEM((nt // 2, depth, 2 * cols), BF),
            pltpu.VMEM((2 * rows, width // 2), BF),
            pltpu.VMEM((2 * rows, width // 2), BF),
            pltpu.VMEM((nt // 2, rows, width), BF),
            pltpu.VMEM((rows, cols), BF),
            pltpu.VMEM((rows, cols), BF),
            pltpu.VMEM((rows, cols), F32),
            dma((3,)), dma((n,)), dma((n,)), dma((n,)), dma((n,)),
            dma((nt // 2,)), dma((nt // 2,)), dma((nt // 2,)), dma((nt // 2,)),
            dma((n,)), dma((n,)), dma((3,)), dma((3,)), dma((3, nt // 2)), dma((3, nt // 2)),
        ],
        compiler_params=pltpu.CompilerParams(
            collective_id=0, has_side_effects=True, vmem_limit_bytes=58 * 2**20
        ),
        name="sublayer",
    )(queries, selected.T, shard_order.reshape(1, n), key_cache, values, out_weight)


def solution(mesh):
    placed = (P("ctx", "tp"), P("ctx", "tp"), P("ctx", "tp"), P("tp", None), P("ctx", None), P())
    return jax.shard_map(
        local, mesh=mesh, in_specs=placed, out_specs=P("ctx", "tp"), check_vma=False
    )
```

```python
import functools
import math

import jax
import jax.numpy as jnp
from jax import lax
from jax.experimental import pallas as pl
from jax.experimental.pallas import tpu as pltpu
from jax.sharding import PartitionSpec as P

DH = 128
TOPK = 3
TILE = 16
CAP = 2
KEYS = 256
UNIT = 4
SCALE = math.log2(math.e) / math.sqrt(DH)
MESH = pl.DeviceIdType.MESH
BF = jnp.bfloat16
F32 = jnp.float32


def iota(shape, dim):
    return lax.broadcasted_iota(jnp.int32, shape, dim)


def dot(a, b):
    return jnp.dot(a, b, preferred_element_type=F32)


def dot_nt(a, b):
    return lax.dot_general(a, b, (((1,), (1,)), ((), ())), preferred_element_type=F32)


def attend(rows, kt, vx, masked):
    count = rows.shape[0]
    scaled = rows.astype(F32) * SCALE
    high = scaled.astype(BF)
    low = (scaled - high.astype(F32)).astype(BF)
    rows = jnp.concatenate([high, low], axis=1)
    steps = vx.shape[0] // KEYS
    peak, total = None, None
    for step in range(steps):
        keys = pl.ds(step * KEYS, KEYS)
        scores = dot(rows, kt[:, keys])
        if masked and step == steps - 1:
            shape = (count, KEYS)
            scores = jnp.where(iota(shape, 1) <= iota(shape, 0) % KEYS, scores, -1e30)
        top = jnp.max(scores, axis=1, keepdims=True)
        if peak is not None:
            top = jnp.maximum(top, peak)
        term = dot(jnp.exp2(scores - top).astype(BF), vx[keys, :])
        total = term if peak is None else total * jnp.exp2(peak - top) + term
        peak = top
    mass = total[:, DH:]
    return total[:, :DH] / mass, peak + jnp.log2(mass)


def kernel(
    n, nt,
    q_ref, sel_ref, order_ref, k_ref, v_ref, w_ref, out_ref,
    kraw, kt, vx, outq, recvq, ret, back, pick, perm, own_mix, own_log,
    wfull, pieces, arrived, ag, term_out, term_in, acc,
    load_sem, qs_sem, qr_sem, bs_sem, br_sem, ws_sem, wr_sem, fs_sem, fr_sem,
    ts_sem, tr_sem, ys_sem, yr_sem, xs_sem, xr_sem,
):
    c = lax.axis_index("ctx")
    t = lax.axis_index("tp")
    core = lax.rem(c, 2)
    sibling = c + 1 - 2 * core
    heads = q_ref.shape[1] // DH
    tiles = sel_ref.shape[1]
    rows = q_ref.shape[0]
    slots = n * CAP
    pair_rows = CAP * TILE
    slot_rows = n * pair_rows
    piece = rows // n
    cols = out_ref.shape[1]
    depth = w_ref.shape[0]
    half = depth // 2

    barrier = pltpu.get_barrier_semaphore()

    def greet_ctx(j, carry):
        pl.semaphore_signal(
            barrier, inc=1, device_id=(lax.rem(c + j, n), t), device_id_type=MESH
        )
        return carry

    for j in range(1, n):
        greet_ctx(j, 0)

    ring = nt // 2
    x, y = t // 2, lax.rem(t, 2)
    across = x * 2 + 1 - y

    def greet_x(j, carry):
        pl.semaphore_signal(
            barrier, inc=1, device_id=(c, lax.rem(x + j, ring) * 2 + y), device_id_type=MESH
        )
        return carry

    lax.fori_loop(1, ring, greet_x, 0)
    pl.semaphore_signal(barrier, inc=1, device_id=(c, across), device_id_type=MESH)

    load_k = pltpu.make_async_copy(k_ref, kraw, load_sem.at[0])
    load_v = pltpu.make_async_copy(v_ref, vx.at[:, pl.ds(0, DH)], load_sem.at[1])
    load_k.start()
    load_v.start()

    slot_shape = (tiles, slots)
    lane = iota(slot_shape, 1)
    square = (tiles, tiles)
    chosen = [
        jnp.sum(
            jnp.where(iota(square, 0) == iota(square, 1), sel_ref[r : r + 1, :].astype(F32), 0.0),
            axis=1,
            keepdims=True,
        ).astype(jnp.int32)
        for r in range(TOPK)
    ]
    named = [(lane // CAP == chosen[r]) for r in range(TOPK)]
    hit = (named[0] | named[1] | named[2]).astype(F32)
    lower = (iota((tiles, tiles), 1) < iota((tiles, tiles), 0)).astype(BF)
    rank = dot(lower, hit.astype(BF))
    right_rank = (rank == (lane % CAP).astype(F32)).astype(F32)
    owner = (hit * right_rank).astype(BF)
    spread = (iota((tiles, rows), 1) // TILE == iota((tiles, rows), 0)).astype(BF)
    block = 256

    def fill(j, carry):
        base = pl.multiple_of(j * block, block)
        row = base + iota((block, slots), 0)
        of_slot = (row // TILE == iota((block, slots), 1)).astype(BF)
        of_tile = dot_nt(of_slot, owner).astype(BF)
        same = iota((block, rows), 0) % TILE == iota((block, rows), 1) % TILE
        gate = jnp.where(same, dot(of_tile, spread), 0.0).astype(BF)
        outq[pl.ds(base, block), :] = dot(gate, q_ref[...]).astype(BF)
        return carry

    lax.fori_loop(0, slot_rows // block, fill, 0)

    pl.semaphore_wait(barrier, n - 1 + ring - 1 + 1)

    def dispatch(k, s, peer=None):
        return pltpu.make_async_remote_copy(
            src_ref=outq.at[pl.ds(pl.multiple_of(k * pair_rows, pair_rows), pair_rows), :],
            dst_ref=recvq.at[s],
            send_sem=qs_sem.at[k],
            recv_sem=qr_sem.at[s],
            device_id=(k if peer is None else peer, t),
            device_id_type=MESH,
        )

    def send_queries(j, carry):
        dispatch(c - 1 - j, c).start()
        return carry

    lax.fori_loop(0, c, send_queries, 0)

    def columns(dest):
        return pl.ds(pl.multiple_of(dest * 2 * cols, 2 * cols), 2 * cols)

    my_half = pl.ds(pl.multiple_of(core * half, half), half)
    its_half = pl.ds(pl.multiple_of((1 - core) * half, half), half)
    weight_load = pltpu.make_async_copy(w_ref.at[:, columns(x)], wfull.at[x], load_sem.at[2])
    weight_load.start()

    def weight_copy(dest):
        return pltpu.make_async_remote_copy(
            src_ref=w_ref.at[my_half, columns(dest)],
            dst_ref=wfull.at[x, my_half, :],
            send_sem=ws_sem.at[dest],
            recv_sem=wr_sem.at[x],
            device_id=(c, dest * 2 + y),
            device_id_type=MESH,
        )

    def weight_arrival(source):
        view = wfull.at[source, my_half, :]
        return pltpu.make_async_remote_copy(
            src_ref=view,
            dst_ref=view,
            send_sem=ws_sem.at[source],
            recv_sem=wr_sem.at[source],
            device_id=(c, source * 2 + y),
            device_id_type=MESH,
        )

    def weight_share(source, rows_of):
        view = wfull.at[source, rows_of, :]
        return pltpu.make_async_remote_copy(
            src_ref=view,
            dst_ref=view,
            send_sem=fs_sem.at[source],
            recv_sem=fr_sem.at[source],
            device_id=(sibling, t),
            device_id_type=MESH,
        )

    def send_weights(j, carry):
        weight_copy(lax.rem(x + j, ring)).start()
        return carry

    lax.fori_loop(1, ring, send_weights, 0)

    recvq[c] = jnp.zeros(recvq.shape[1:], BF)

    def clear(k, carry):
        back[k] = jnp.zeros(back.shape[1:], BF)
        return carry

    lax.fori_loop(c, n, clear, 0)

    for r in range(TOPK):
        mine = (named[r].astype(F32) * right_rank).astype(BF)
        of_row = dot(
            (iota((rows, tiles), 0) // TILE == iota((rows, tiles), 1)).astype(BF), mine
        ).astype(BF)
        to_slot = (iota((slots, slot_rows), 1) // TILE == iota((slots, slot_rows), 0)).astype(BF)
        same = iota((rows, slot_rows), 0) % TILE == iota((rows, slot_rows), 1) % TILE
        pick[r * rows : (r + 1) * rows, :] = jnp.where(same, dot(of_row, to_slot), 0.0).astype(BF)
    wanted = (iota((n, n), 0) == order_ref[...]).astype(BF)
    row2 = iota((2 * rows, n), 0)
    of_shard = (row2 // (2 * piece) == iota((2 * rows, n), 1)).astype(BF)
    of_piece = dot_nt(of_shard, wanted).astype(BF)
    to_rows = (iota((n, rows), 1) // piece == iota((n, rows), 0)).astype(BF)
    same = iota((2 * rows, rows), 0) % piece == iota((2 * rows, rows), 1) % piece
    perm[...] = jnp.where(same, dot(of_piece, to_rows), 0.0).astype(BF)

    load_k.wait()
    kt[0:DH, :] = kraw[...].T
    kt[DH:, :] = kt[0:DH, :]
    load_v.wait()
    vx[:, DH:] = jnp.ones((vx.shape[0], DH), BF)

    for first in range(0, heads, 2):
        pair = jnp.concatenate(
            [q_ref[:, h * DH : (h + 1) * DH] for h in (first, first + 1)], axis=0
        )
        mix, log_mass = attend(pair, kt, vx, True)
        for i, h in enumerate((first, first + 1)):
            own_mix[:, h * DH : (h + 1) * DH] = mix[i * rows : (i + 1) * rows]
            own_log[:, h * DH : (h + 1) * DH] = log_mass[i * rows : (i + 1) * rows]

    def give_back(s, k, peer=None):
        return pltpu.make_async_remote_copy(
            src_ref=ret.at[s],
            dst_ref=back.at[k],
            send_sem=bs_sem.at[s],
            recv_sem=br_sem.at[k],
            device_id=(s if peer is None else peer, t),
            device_id_type=MESH,
        )

    def serve(g, carry):
        names = []
        for u in range(UNIT):
            s = c + 1 + g * UNIT + u
            names.append((s, jnp.where(s < n, s, c)))

            @pl.when(s < n)
            def _():
                dispatch(c, s, s).wait_recv()

        parts = []
        for s, at in names:
            held = recvq[at]
            parts += [held[:, h * DH : (h + 1) * DH] for h in range(heads)]
        mix, log_mass = attend(jnp.concatenate(parts, axis=0), kt, vx, False)
        spot = iota((TILE, DH), 1)
        for u, (s, at) in enumerate(names):
            base = u * heads * pair_rows
            ret[at, : heads * pair_rows, :] = mix[base : base + heads * pair_rows].astype(BF)
            stat = jnp.zeros((TILE, DH), F32)
            for i in range(CAP):
                for h in range(heads):
                    first = base + h * pair_rows + i * TILE
                    here = (spot // (3 * heads) == i) & (spot % heads == h)
                    stat = jnp.where(here, log_mass[first : first + TILE], stat)
            high = stat.astype(BF).astype(F32)
            middle = (stat - high).astype(BF).astype(F32)
            low = stat - high - middle
            part = spot % (3 * heads) // heads
            packed = jnp.where(part == 0, high, jnp.where(part == 1, middle, low))
            ret[at, heads * pair_rows :, :] = packed.astype(BF)

            @pl.when(s < n)
            def _():
                give_back(s, c).start()

        return carry

    groups = (n - 1 - c + UNIT - 1) // UNIT
    turn = jnp.minimum(groups, (c + 11) // UNIT)
    lax.fori_loop(0, turn, serve, 0)

    def await_back(j, carry):
        give_back(c, c - 1 - j, c - 1 - j).wait_recv()
        return carry

    lax.fori_loop(0, c, await_back, 0)
    to_heads = (
        (iota((DH, heads * DH), 0) % heads == iota((DH, heads * DH), 1) // DH)
        & (iota((DH, heads * DH), 0) < 3 * heads * CAP)
    ).astype(BF)
    row_of = (iota((rows, tiles), 0) // TILE == iota((rows, tiles), 1)).astype(BF)
    stats = back[:, heads * pair_rows :, :]
    stat_lane = iota(stats.shape, 2) // (3 * heads)
    stats = jnp.concatenate(
        [jnp.where(stat_lane == i, stats.astype(F32), 0.0).astype(BF) for i in range(CAP)], axis=1
    ).reshape(slot_rows, DH)
    wide = [
        back[:, h * pair_rows : (h + 1) * pair_rows, :].reshape(slot_rows, DH) for h in range(heads)
    ]
    taken = dot(pick[...], jnp.concatenate(wide, axis=1))
    taken_log = dot(dot(pick[...], stats).astype(BF), to_heads)
    logs, mixes = [own_log[...]], [own_mix[...]]
    for r in range(TOPK):
        some = slice(r * rows, (r + 1) * rows)
        live = dot(row_of, jnp.broadcast_to((chosen[r] >= 0).astype(F32), (tiles, heads * DH)).astype(BF))
        logs.append(jnp.where(live > 0.5, taken_log[some], -1e30))
        mixes.append(taken[some])
    top = jnp.maximum(jnp.maximum(logs[0], logs[1]), jnp.maximum(logs[2], logs[3]))
    numerator, denominator = 0.0, 0.0
    for log_mass, mix in zip(logs, mixes):
        weight = jnp.exp2(log_mass - top)
        numerator = numerator + weight * mix
        denominator = denominator + weight
    attention = (numerator / denominator).astype(BF)

    mid = heads * DH // 2
    left = dot(perm[...], attention[:, :mid])
    right = dot(perm[...], attention[:, mid:])
    side = iota((2 * rows, mid), 0) // piece % 2
    pieces[...] = jnp.where(side == 0, left, right).astype(BF)
    size = 2 * piece

    def deliver(d, s):
        return pltpu.make_async_remote_copy(
            src_ref=pieces.at[pl.ds(pl.multiple_of(d * size, size), size), :],
            dst_ref=arrived.at[pl.ds(pl.multiple_of(s * size, size), size), :],
            send_sem=ts_sem.at[d],
            recv_sem=tr_sem.at[s],
            device_id=(d, t),
            device_id_type=MESH,
        )

    def send_piece(j, carry):
        deliver(lax.rem(c + j, n), c).start()
        return carry

    for j in range(1, n):
        send_piece(j, 0)
    here = pl.ds(pl.multiple_of(c * size, size), size)
    arrived[here, :] = pieces[here, :]

    lax.fori_loop(turn, groups, serve, 0)

    def share(j, carry):
        source = lax.rem(x + j, ring)
        weight_arrival(source).wait_recv()
        weight_share(source, my_half).start()
        return carry

    lax.fori_loop(1, ring, share, 0)

    def await_piece(s, carry):
        view = arrived.at[pl.ds(pl.multiple_of(s * size, size), size), :]

        @pl.when(s != c)
        def _():
            pltpu.make_async_remote_copy(
                src_ref=view,
                dst_ref=view,
                send_sem=ts_sem.at[s],
                recv_sem=tr_sem.at[s],
                device_id=(s, t),
                device_id_type=MESH,
            ).wait_recv()

        return carry

    def head_copy(g, which, send, peer):
        begin, count = bounds[g]
        view = ag.at[which, pl.ds(begin * piece, count * piece), :]
        return pltpu.make_async_remote_copy(
            src_ref=view,
            dst_ref=view,
            send_sem=xs_sem.at[g, send],
            recv_sem=xr_sem.at[g, which],
            device_id=(c, peer * 2 + y),
            device_id_type=MESH,
        )

    def term_copy(g):
        begin, count = bounds[g]
        some = pl.ds(begin * piece, count * piece)
        return pltpu.make_async_remote_copy(
            src_ref=term_out.at[some, :],
            dst_ref=term_in.at[some, :],
            send_sem=ys_sem.at[g],
            recv_sem=yr_sem.at[g],
            device_id=(c, across),
            device_id_type=MESH,
        )

    def gather_heads(g):
        begin, count = bounds[g]
        lax.fori_loop(begin, begin + count, await_piece, 0)
        split = arrived[begin * size : (begin + count) * size, :].astype(F32)
        split = split.reshape(count, 2, piece, mid)
        some = slice(begin * piece, (begin + count) * piece)
        ag[x, some, :mid] = split[:, 0].reshape(count * piece, mid).astype(BF)
        ag[x, some, mid:] = split[:, 1].reshape(count * piece, mid).astype(BF)
        for j in range(1, ring):
            dest = lax.rem(x + j, ring)
            head_copy(g, x, dest, dest).start()

    def term(some, half_y):
        where = pl.ds(pl.multiple_of(half_y * cols, cols), cols)
        total = dot(ag[0, some, :], wfull[0, :, where])
        for source in range(1, ring):
            total = total + dot(ag[source, some, :], wfull[source, :, where])
        return total

    def project(g):
        begin, count = bounds[g]
        some = slice(begin * piece, (begin + count) * piece)
        for j in range(1, ring):
            source = lax.rem(x + j, ring)
            head_copy(g, source, source, source).wait_recv()

        term_out[some, :] = term(some, 1 - y).astype(BF)
        term_copy(g).start()

    def finish(g):
        begin, count = bounds[g]
        some = slice(begin * piece, (begin + count) * piece)
        term_copy(g).wait_recv()
        out_ref[some, :] = (acc[some, :] + term_in[some, :].astype(F32)).astype(BF)

    bounds = ((0, n // 2), (n // 2, n // 4), (n * 3 // 4, n // 4))
    def drain_queries(k, carry):
        dispatch(k, c).wait_send()
        return carry

    lax.fori_loop(0, c, drain_queries, 0)

    def drain_back(s, carry):
        give_back(s, c).wait_send()
        return carry

    lax.fori_loop(c + 1, n, drain_back, 0)
    gather_heads(0)
    weight_load.wait()

    def await_weights(j, carry):
        weight_share(lax.rem(x + j, ring), its_half).wait_recv()
        return carry

    lax.fori_loop(1, ring, await_weights, 0)
    gather_heads(1)
    project(0)
    gather_heads(2)
    project(1)
    project(2)
    def drain_ctx(j, carry):
        deliver(lax.rem(c + j, n), c).wait_send()
        return carry

    lax.fori_loop(1, n, drain_ctx, 0)
    acc[...] = term(slice(0, rows), y)
    for g in range(len(bounds)):
        finish(g)

    for g in range(len(bounds)):
        term_copy(g).wait_send()
        for j in range(1, ring):
            dest = lax.rem(x + j, ring)
            head_copy(g, x, dest, dest).wait_send()

    def drain_weights(j, carry):
        peer = lax.rem(x + j, ring)
        weight_copy(peer).wait_send()
        weight_share(peer, my_half).wait_send()
        return carry

    lax.fori_loop(1, ring, drain_weights, 0)


def local(queries, key_cache, values, out_weight, selected, shard_order):
    n, nt = lax.axis_size("ctx"), lax.axis_size("tp")
    rows, width = queries.shape
    keys = key_cache.shape[0]
    depth, model = out_weight.shape
    cols = model // nt
    pair_rows = CAP * TILE
    heads = width // DH
    dma = pltpu.SemaphoreType.DMA
    vmem = pl.BlockSpec(memory_space=pltpu.VMEM)
    hbm = pl.BlockSpec(memory_space=pl.ANY)
    return pl.pallas_call(
        functools.partial(kernel, n, nt),
        out_shape=jax.ShapeDtypeStruct((rows, cols), BF),
        in_specs=[vmem, vmem, vmem, hbm, hbm, hbm],
        out_specs=vmem,
        scratch_shapes=[
            pltpu.VMEM((keys, DH), BF),
            pltpu.VMEM((2 * DH, keys), BF),
            pltpu.VMEM((keys, 2 * DH), BF),
            pltpu.VMEM((n * pair_rows, width), BF),
            pltpu.VMEM((n, pair_rows, width), BF),
            pltpu.VMEM((n, heads * pair_rows + TILE, DH), BF),
            pltpu.VMEM((n, heads * pair_rows + TILE, DH), BF),
            pltpu.VMEM((TOPK * rows, n * pair_rows), BF),
            pltpu.VMEM((2 * rows, rows), BF),
            pltpu.VMEM((rows, width), F32),
            pltpu.VMEM((rows, width), F32),
            pltpu.VMEM((nt // 2, depth, 2 * cols), BF),
            pltpu.VMEM((2 * rows, width // 2), BF),
            pltpu.VMEM((2 * rows, width // 2), BF),
            pltpu.VMEM((nt // 2, rows, width), BF),
            pltpu.VMEM((rows, cols), BF),
            pltpu.VMEM((rows, cols), BF),
            pltpu.VMEM((rows, cols), F32),
            dma((3,)), dma((n,)), dma((n,)), dma((n,)), dma((n,)),
            dma((nt // 2,)), dma((nt // 2,)), dma((nt // 2,)), dma((nt // 2,)),
            dma((n,)), dma((n,)), dma((3,)), dma((3,)), dma((3, nt // 2)), dma((3, nt // 2)),
        ],
        compiler_params=pltpu.CompilerParams(
            collective_id=0, has_side_effects=True, vmem_limit_bytes=58 * 2**20
        ),
        name="sublayer",
    )(queries, selected.T, shard_order.reshape(1, n), key_cache, values, out_weight)


def solution(mesh):
    placed = (P("ctx", "tp"), P("ctx", "tp"), P("ctx", "tp"), P("tp", None), P("ctx", None), P())
    return jax.shard_map(
        local, mesh=mesh, in_specs=placed, out_specs=P("ctx", "tp"), check_vma=False
    )
```

```python
import functools
import math

import jax
import jax.numpy as jnp
from jax import lax
from jax.experimental import pallas as pl
from jax.experimental.pallas import tpu as pltpu
from jax.sharding import PartitionSpec as P

DH = 128
TOPK = 3
TILE = 16
CAP = 2
KEYS = 256
UNIT = 4
SCALE = math.log2(math.e) / math.sqrt(DH)
MESH = pl.DeviceIdType.MESH
BF = jnp.bfloat16
F32 = jnp.float32


def iota(shape, dim):
    return lax.broadcasted_iota(jnp.int32, shape, dim)


def dot(a, b):
    return jnp.dot(a, b, preferred_element_type=F32)


def dot_nt(a, b):
    return lax.dot_general(a, b, (((1,), (1,)), ((), ())), preferred_element_type=F32)


def attend(rows, kt, vx, masked):
    count = rows.shape[0]
    scaled = rows.astype(F32) * SCALE
    high = scaled.astype(BF)
    low = (scaled - high.astype(F32)).astype(BF)
    rows = jnp.concatenate([high, low], axis=1)
    steps = vx.shape[0] // KEYS
    peak, total = None, None
    for step in range(steps):
        keys = pl.ds(step * KEYS, KEYS)
        scores = dot(rows, kt[:, keys])
        if masked and step == steps - 1:
            shape = (count, KEYS)
            scores = jnp.where(iota(shape, 1) <= iota(shape, 0) % KEYS, scores, -1e30)
        top = jnp.max(scores, axis=1, keepdims=True)
        if peak is not None:
            top = jnp.maximum(top, peak)
        term = dot(jnp.exp2(scores - top).astype(BF), vx[keys, :])
        total = term if peak is None else total * jnp.exp2(peak - top) + term
        peak = top
    mass = total[:, DH:]
    return total[:, :DH] / mass, peak + jnp.log2(mass)


def kernel(
    n, nt,
    q_ref, sel_ref, order_ref, k_ref, v_ref, w_ref, out_ref,
    kraw, kt, vx, outq, recvq, ret, back, pick, perm, own_mix, own_log,
    wfull, pieces, arrived, ag, term_out, term_in, acc,
    load_sem, qs_sem, qr_sem, bs_sem, br_sem, ws_sem, wr_sem, fs_sem, fr_sem,
    ts_sem, tr_sem, ys_sem, yr_sem, xs_sem, xr_sem,
):
    c = lax.axis_index("ctx")
    t = lax.axis_index("tp")
    core = lax.rem(c, 2)
    sibling = c + 1 - 2 * core
    heads = q_ref.shape[1] // DH
    tiles = sel_ref.shape[1]
    rows = q_ref.shape[0]
    slots = n * CAP
    pair_rows = CAP * TILE
    slot_rows = n * pair_rows
    piece = rows // n
    cols = out_ref.shape[1]
    depth = w_ref.shape[0]
    half = depth // 2

    barrier = pltpu.get_barrier_semaphore()

    def greet_ctx(j, carry):
        pl.semaphore_signal(
            barrier, inc=1, device_id=(lax.rem(c + j, n), t), device_id_type=MESH
        )
        return carry

    for j in range(1, n):
        greet_ctx(j, 0)

    ring = nt // 2
    x, y = t // 2, lax.rem(t, 2)
    across = x * 2 + 1 - y

    def greet_x(j, carry):
        pl.semaphore_signal(
            barrier, inc=1, device_id=(c, lax.rem(x + j, ring) * 2 + y), device_id_type=MESH
        )
        return carry

    lax.fori_loop(1, ring, greet_x, 0)
    pl.semaphore_signal(barrier, inc=1, device_id=(c, across), device_id_type=MESH)

    load_k = pltpu.make_async_copy(k_ref, kraw, load_sem.at[0])
    load_v = pltpu.make_async_copy(v_ref, vx.at[:, pl.ds(0, DH)], load_sem.at[1])
    load_k.start()
    load_v.start()

    slot_shape = (tiles, slots)
    lane = iota(slot_shape, 1)
    square = (tiles, tiles)
    chosen = [
        jnp.sum(
            jnp.where(iota(square, 0) == iota(square, 1), sel_ref[r : r + 1, :].astype(F32), 0.0),
            axis=1,
            keepdims=True,
        ).astype(jnp.int32)
        for r in range(TOPK)
    ]
    named = [(lane // CAP == chosen[r]) for r in range(TOPK)]
    hit = (named[0] | named[1] | named[2]).astype(F32)
    lower = (iota((tiles, tiles), 1) < iota((tiles, tiles), 0)).astype(BF)
    rank = dot(lower, hit.astype(BF))
    right_rank = (rank == (lane % CAP).astype(F32)).astype(F32)
    owner = (hit * right_rank).astype(BF)
    spread = (iota((tiles, rows), 1) // TILE == iota((tiles, rows), 0)).astype(BF)
    block = 256

    def fill(j, carry):
        base = pl.multiple_of(j * block, block)
        row = base + iota((block, slots), 0)
        of_slot = (row // TILE == iota((block, slots), 1)).astype(BF)
        of_tile = dot_nt(of_slot, owner).astype(BF)
        same = iota((block, rows), 0) % TILE == iota((block, rows), 1) % TILE
        gate = jnp.where(same, dot(of_tile, spread), 0.0).astype(BF)
        outq[pl.ds(base, block), :] = dot(gate, q_ref[...]).astype(BF)
        return carry

    lax.fori_loop(0, slot_rows // block, fill, 0)

    pl.semaphore_wait(barrier, n - 1 + ring - 1 + 1)

    def dispatch(k, s, peer=None):
        return pltpu.make_async_remote_copy(
            src_ref=outq.at[pl.ds(pl.multiple_of(k * pair_rows, pair_rows), pair_rows), :],
            dst_ref=recvq.at[s],
            send_sem=qs_sem.at[k],
            recv_sem=qr_sem.at[s],
            device_id=(k if peer is None else peer, t),
            device_id_type=MESH,
        )

    def send_queries(j, carry):
        dispatch(c - 1 - j, c).start()
        return carry

    lax.fori_loop(0, c, send_queries, 0)

    def columns(dest):
        return pl.ds(pl.multiple_of(dest * 2 * cols, 2 * cols), 2 * cols)

    my_half = pl.ds(pl.multiple_of(core * half, half), half)
    its_half = pl.ds(pl.multiple_of((1 - core) * half, half), half)
    weight_load = pltpu.make_async_copy(w_ref.at[:, columns(x)], wfull.at[x], load_sem.at[2])
    weight_load.start()

    def weight_copy(dest):
        return pltpu.make_async_remote_copy(
            src_ref=w_ref.at[my_half, columns(dest)],
            dst_ref=wfull.at[x, my_half, :],
            send_sem=ws_sem.at[dest],
            recv_sem=wr_sem.at[x],
            device_id=(c, dest * 2 + y),
            device_id_type=MESH,
        )

    def weight_arrival(source):
        view = wfull.at[source, my_half, :]
        return pltpu.make_async_remote_copy(
            src_ref=view,
            dst_ref=view,
            send_sem=ws_sem.at[source],
            recv_sem=wr_sem.at[source],
            device_id=(c, source * 2 + y),
            device_id_type=MESH,
        )

    def weight_share(source, rows_of):
        view = wfull.at[source, rows_of, :]
        return pltpu.make_async_remote_copy(
            src_ref=view,
            dst_ref=view,
            send_sem=fs_sem.at[source],
            recv_sem=fr_sem.at[source],
            device_id=(sibling, t),
            device_id_type=MESH,
        )

    def send_weights(j, carry):
        weight_copy(lax.rem(x + j, ring)).start()
        return carry

    lax.fori_loop(1, ring, send_weights, 0)

    recvq[c] = jnp.zeros(recvq.shape[1:], BF)

    def clear(k, carry):
        back[k] = jnp.zeros(back.shape[1:], BF)
        return carry

    lax.fori_loop(c, n, clear, 0)

    for r in range(TOPK):
        mine = (named[r].astype(F32) * right_rank).astype(BF)
        of_row = dot(
            (iota((rows, tiles), 0) // TILE == iota((rows, tiles), 1)).astype(BF), mine
        ).astype(BF)
        to_slot = (iota((slots, slot_rows), 1) // TILE == iota((slots, slot_rows), 0)).astype(BF)
        same = iota((rows, slot_rows), 0) % TILE == iota((rows, slot_rows), 1) % TILE
        pick[r * rows : (r + 1) * rows, :] = jnp.where(same, dot(of_row, to_slot), 0.0).astype(BF)
    wanted = (iota((n, n), 0) == order_ref[...]).astype(BF)
    row2 = iota((2 * rows, n), 0)
    of_shard = (row2 // (2 * piece) == iota((2 * rows, n), 1)).astype(BF)
    of_piece = dot_nt(of_shard, wanted).astype(BF)
    to_rows = (iota((n, rows), 1) // piece == iota((n, rows), 0)).astype(BF)
    same = iota((2 * rows, rows), 0) % piece == iota((2 * rows, rows), 1) % piece
    perm[...] = jnp.where(same, dot(of_piece, to_rows), 0.0).astype(BF)

    load_k.wait()
    kt[0:DH, :] = kraw[...].T
    kt[DH:, :] = kt[0:DH, :]
    load_v.wait()
    vx[:, DH:] = jnp.ones((vx.shape[0], DH), BF)

    for first in range(0, heads, 2):
        pair = jnp.concatenate(
            [q_ref[:, h * DH : (h + 1) * DH] for h in (first, first + 1)], axis=0
        )
        mix, log_mass = attend(pair, kt, vx, True)
        for i, h in enumerate((first, first + 1)):
            own_mix[:, h * DH : (h + 1) * DH] = mix[i * rows : (i + 1) * rows]
            own_log[:, h * DH : (h + 1) * DH] = log_mass[i * rows : (i + 1) * rows]

    def give_back(s, k, peer=None):
        return pltpu.make_async_remote_copy(
            src_ref=ret.at[s],
            dst_ref=back.at[k],
            send_sem=bs_sem.at[s],
            recv_sem=br_sem.at[k],
            device_id=(s if peer is None else peer, t),
            device_id_type=MESH,
        )

    def serve(g, carry):
        names = []
        for u in range(UNIT):
            s = c + 1 + g * UNIT + u
            names.append((s, jnp.where(s < n, s, c)))

            @pl.when(s < n)
            def _():
                dispatch(c, s, s).wait_recv()

        parts = []
        for s, at in names:
            held = recvq[at]
            parts += [held[:, h * DH : (h + 1) * DH] for h in range(heads)]
        mix, log_mass = attend(jnp.concatenate(parts, axis=0), kt, vx, False)
        spot = iota((TILE, DH), 1)
        for u, (s, at) in enumerate(names):
            base = u * heads * pair_rows
            ret[at, : heads * pair_rows, :] = mix[base : base + heads * pair_rows].astype(BF)
            stat = jnp.zeros((TILE, DH), F32)
            for i in range(CAP):
                for h in range(heads):
                    first = base + h * pair_rows + i * TILE
                    here = (spot // (3 * heads) == i) & (spot % heads == h)
                    stat = jnp.where(here, log_mass[first : first + TILE], stat)
            high = stat.astype(BF).astype(F32)
            middle = (stat - high).astype(BF).astype(F32)
            low = stat - high - middle
            part = spot % (3 * heads) // heads
            packed = jnp.where(part == 0, high, jnp.where(part == 1, middle, low))
            ret[at, heads * pair_rows :, :] = packed.astype(BF)

            @pl.when(s < n)
            def _():
                give_back(s, c).start()

        return carry

    groups = (n - 1 - c + UNIT - 1) // UNIT
    turn = jnp.minimum(groups, (c + 11) // UNIT)
    lax.fori_loop(0, turn, serve, 0)

    def await_back(j, carry):
        give_back(c, c - 1 - j, c - 1 - j).wait_recv()
        return carry

    lax.fori_loop(0, c, await_back, 0)
    to_heads = (
        (iota((DH, heads * DH), 0) % heads == iota((DH, heads * DH), 1) // DH)
        & (iota((DH, heads * DH), 0) < 3 * heads * CAP)
    ).astype(BF)
    row_of = (iota((rows, tiles), 0) // TILE == iota((rows, tiles), 1)).astype(BF)
    stats = back[:, heads * pair_rows :, :]
    stat_lane = iota(stats.shape, 2) // (3 * heads)
    stats = jnp.concatenate(
        [jnp.where(stat_lane == i, stats.astype(F32), 0.0).astype(BF) for i in range(CAP)], axis=1
    ).reshape(slot_rows, DH)
    wide = [
        back[:, h * pair_rows : (h + 1) * pair_rows, :].reshape(slot_rows, DH) for h in range(heads)
    ]
    taken = dot(pick[...], jnp.concatenate(wide, axis=1))
    taken_log = dot(dot(pick[...], stats).astype(BF), to_heads)
    logs, mixes = [own_log[...]], [own_mix[...]]
    for r in range(TOPK):
        some = slice(r * rows, (r + 1) * rows)
        live = dot(row_of, jnp.broadcast_to((chosen[r] >= 0).astype(F32), (tiles, heads * DH)).astype(BF))
        logs.append(jnp.where(live > 0.5, taken_log[some], -1e30))
        mixes.append(taken[some])
    top = jnp.maximum(jnp.maximum(logs[0], logs[1]), jnp.maximum(logs[2], logs[3]))
    numerator, denominator = 0.0, 0.0
    for log_mass, mix in zip(logs, mixes):
        weight = jnp.exp2(log_mass - top)
        numerator = numerator + weight * mix
        denominator = denominator + weight
    attention = (numerator / denominator).astype(BF)

    mid = heads * DH // 2
    left = dot(perm[...], attention[:, :mid])
    right = dot(perm[...], attention[:, mid:])
    side = iota((2 * rows, mid), 0) // piece % 2
    pieces[...] = jnp.where(side == 0, left, right).astype(BF)
    size = 2 * piece

    def deliver(d, s):
        return pltpu.make_async_remote_copy(
            src_ref=pieces.at[pl.ds(pl.multiple_of(d * size, size), size), :],
            dst_ref=arrived.at[pl.ds(pl.multiple_of(s * size, size), size), :],
            send_sem=ts_sem.at[d],
            recv_sem=tr_sem.at[s],
            device_id=(d, t),
            device_id_type=MESH,
        )

    def send_piece(j, carry):
        deliver(lax.rem(c + j, n), c).start()
        return carry

    for j in range(1, n):
        send_piece(j, 0)
    here = pl.ds(pl.multiple_of(c * size, size), size)
    arrived[here, :] = pieces[here, :]

    lax.fori_loop(turn, groups, serve, 0)

    def share(j, carry):
        source = lax.rem(x + j, ring)
        weight_arrival(source).wait_recv()
        weight_share(source, my_half).start()
        return carry

    lax.fori_loop(1, ring, share, 0)

    def await_piece(s, carry):
        view = arrived.at[pl.ds(pl.multiple_of(s * size, size), size), :]

        @pl.when(s != c)
        def _():
            pltpu.make_async_remote_copy(
                src_ref=view,
                dst_ref=view,
                send_sem=ts_sem.at[s],
                recv_sem=tr_sem.at[s],
                device_id=(s, t),
                device_id_type=MESH,
            ).wait_recv()

        return carry

    def head_copy(g, which, send, peer):
        begin, count = bounds[g]
        view = ag.at[which, pl.ds(begin * piece, count * piece), :]
        return pltpu.make_async_remote_copy(
            src_ref=view,
            dst_ref=view,
            send_sem=xs_sem.at[g, send],
            recv_sem=xr_sem.at[g, which],
            device_id=(c, peer * 2 + y),
            device_id_type=MESH,
        )

    def term_copy(g):
        begin, count = bounds[g]
        some = pl.ds(begin * piece, count * piece)
        return pltpu.make_async_remote_copy(
            src_ref=term_out.at[some, :],
            dst_ref=term_in.at[some, :],
            send_sem=ys_sem.at[g],
            recv_sem=yr_sem.at[g],
            device_id=(c, across),
            device_id_type=MESH,
        )

    def gather_heads(g):
        begin, count = bounds[g]
        lax.fori_loop(begin, begin + count, await_piece, 0)
        split = arrived[begin * size : (begin + count) * size, :].astype(F32)
        split = split.reshape(count, 2, piece, mid)
        some = slice(begin * piece, (begin + count) * piece)
        ag[x, some, :mid] = split[:, 0].reshape(count * piece, mid).astype(BF)
        ag[x, some, mid:] = split[:, 1].reshape(count * piece, mid).astype(BF)
        for j in range(1, ring):
            dest = lax.rem(x + j, ring)
            head_copy(g, x, dest, dest).start()

    def project(g):
        begin, count = bounds[g]
        some = slice(begin * piece, (begin + count) * piece)
        for j in range(1, ring):
            source = lax.rem(x + j, ring)
            head_copy(g, source, source, source).wait_recv()

        def term(half_y):
            where = pl.ds(pl.multiple_of(half_y * cols, cols), cols)
            total = dot(ag[0, some, :], wfull[0, :, where])
            for source in range(1, ring):
                total = total + dot(ag[source, some, :], wfull[source, :, where])
            return total

        term_out[some, :] = term(1 - y).astype(BF)
        term_copy(g).start()
        acc[some, :] = term(y)

    def finish(g):
        begin, count = bounds[g]
        some = slice(begin * piece, (begin + count) * piece)
        term_copy(g).wait_recv()
        out_ref[some, :] = (acc[some, :] + term_in[some, :].astype(F32)).astype(BF)

    cuts = (0, n * 9 // 16, n * 13 // 16, n)
    bounds = tuple((a, b - a) for a, b in zip(cuts, cuts[1:]))
    def drain_queries(k, carry):
        dispatch(k, c).wait_send()
        return carry

    lax.fori_loop(0, c, drain_queries, 0)

    def drain_back(s, carry):
        give_back(s, c).wait_send()
        return carry

    lax.fori_loop(c + 1, n, drain_back, 0)
    gather_heads(0)
    weight_load.wait()

    def await_weights(j, carry):
        weight_share(lax.rem(x + j, ring), its_half).wait_recv()
        return carry

    lax.fori_loop(1, ring, await_weights, 0)
    gather_heads(1)
    project(0)
    gather_heads(2)
    def drain_ctx(j, carry):
        deliver(lax.rem(c + j, n), c).wait_send()
        return carry

    lax.fori_loop(1, n, drain_ctx, 0)
    project(1)
    project(2)
    for g in range(len(bounds)):
        finish(g)

    for g in range(len(bounds)):
        term_copy(g).wait_send()
        for j in range(1, ring):
            dest = lax.rem(x + j, ring)
            head_copy(g, x, dest, dest).wait_send()

    def drain_weights(j, carry):
        peer = lax.rem(x + j, ring)
        weight_copy(peer).wait_send()
        weight_share(peer, my_half).wait_send()
        return carry

    lax.fori_loop(1, ring, drain_weights, 0)


def local(queries, key_cache, values, out_weight, selected, shard_order):
    n, nt = lax.axis_size("ctx"), lax.axis_size("tp")
    rows, width = queries.shape
    keys = key_cache.shape[0]
    depth, model = out_weight.shape
    cols = model // nt
    pair_rows = CAP * TILE
    heads = width // DH
    dma = pltpu.SemaphoreType.DMA
    vmem = pl.BlockSpec(memory_space=pltpu.VMEM)
    hbm = pl.BlockSpec(memory_space=pl.ANY)
    return pl.pallas_call(
        functools.partial(kernel, n, nt),
        out_shape=jax.ShapeDtypeStruct((rows, cols), BF),
        in_specs=[vmem, vmem, vmem, hbm, hbm, hbm],
        out_specs=vmem,
        scratch_shapes=[
            pltpu.VMEM((keys, DH), BF),
            pltpu.VMEM((2 * DH, keys), BF),
            pltpu.VMEM((keys, 2 * DH), BF),
            pltpu.VMEM((n * pair_rows, width), BF),
            pltpu.VMEM((n, pair_rows, width), BF),
            pltpu.VMEM((n, heads * pair_rows + TILE, DH), BF),
            pltpu.VMEM((n, heads * pair_rows + TILE, DH), BF),
            pltpu.VMEM((TOPK * rows, n * pair_rows), BF),
            pltpu.VMEM((2 * rows, rows), BF),
            pltpu.VMEM((rows, width), F32),
            pltpu.VMEM((rows, width), F32),
            pltpu.VMEM((nt // 2, depth, 2 * cols), BF),
            pltpu.VMEM((2 * rows, width // 2), BF),
            pltpu.VMEM((2 * rows, width // 2), BF),
            pltpu.VMEM((nt // 2, rows, width), BF),
            pltpu.VMEM((rows, cols), BF),
            pltpu.VMEM((rows, cols), BF),
            pltpu.VMEM((rows, cols), F32),
            dma((3,)), dma((n,)), dma((n,)), dma((n,)), dma((n,)),
            dma((nt // 2,)), dma((nt // 2,)), dma((nt // 2,)), dma((nt // 2,)),
            dma((n,)), dma((n,)), dma((3,)), dma((3,)), dma((3, nt // 2)), dma((3, nt // 2)),
        ],
        compiler_params=pltpu.CompilerParams(
            collective_id=0, has_side_effects=True, vmem_limit_bytes=58 * 2**20
        ),
        name="sublayer",
    )(queries, selected.T, shard_order.reshape(1, n), key_cache, values, out_weight)


def solution(mesh):
    placed = (P("ctx", "tp"), P("ctx", "tp"), P("ctx", "tp"), P("tp", None), P("ctx", None), P())
    return jax.shard_map(
        local, mesh=mesh, in_specs=placed, out_specs=P("ctx", "tp"), check_vma=False
    )
```
